128 devices in a mesh: task: 4 (over x), patch: 32 (over z, y, core).
Axes of the slice: x: 4, y: 4, z: 4, core: 2. Of those that a mesh axis runs over, the one named last changes fastest.
Arguments:
- trials_initial_dye: float32 [64, 4, 256, 1024], P('task', None, 'patch'), may hold values from -6 to 6
- diffusivity: float32 [4], replicated, may hold values from 0.02 to 0.2
- wet_mask: int32 [256, 1024], P('patch'), may hold values 0 or 1
- deeper_donor_tier: int32 [4, 256, 1024], P(None, 'patch'), may hold values from 0 to 2
- shallower_tier_fraction: float32 [4, 256, 1024], P(None, 'patch'), may hold values from 0 to 1
- obs_pos: int32 [262144], P('patch'), may hold values from 0 to 8191, as said below
- obs_value: float32 [262144], P('patch'), may hold values from -6 to 6
- obs_var: float32 [262144], P('patch'), may hold values from 0.5 to 2
- observation_list: int32 [64, 256, 32], P('patch', 'task'), may hold values from 0 to 262143, as said below
- obs_count: int32 [64, 256], P('patch', 'task'), may hold values from 1 to 32, as said below
Outputs:
- analysis: float32 [64, 4, 256, 1024], P('task', None, 'patch')
The draws below stay inside these ranges and needn't reach their ends.
Inputs may be any that keep to these rules, and one draw needn't show every extreme that they name: `obs_pos`: observation k of strip s (entry s * 8192 + k) lies in column k // 8 of the strip; the entry is its row within the strip times 1024 plus that column. `observation_list`: each listed observation lies in a strip at most two strips from the coarse point's strip and in a column at most 4 columns from the point's block's first column; entries may repeat. `obs_count`: slots at and beyond the count are ignored.
All inputs are finite; a program needn't handle non-finite values. No bound on the sum of `wet_mask` on one device may be relied on, other than what follows from the above.
Results may differ from the reference program's by a relative error of at most 0.0003.
Values sent between devices are 32-bit elements; how exact they have to be, the bound alone decides.
A program may use at most 384 MiB of HBM per device.

```python
import math
import jax
import jax.numpy as jnp
from jax import lax

EASTWARD_CELLS = 1024
ROWS = 8
LEV = 4
STEPS = 4
COARSE = 4
OBS_DEV = 8192
OBS_PT = 32
LOC = 24
NS_ITERS = 6
ENSEMBLE = 64
NORTHWARD_CELLS = 256
NYC = 64
NXC = 256
OBS = 262144


def draw_obs_pos(key, part):
    key = jax.random.fold_in(key, 11)
    total_obs = OBS_DEV * (NORTHWARD_CELLS // ROWS)
    rows_drawn = jax.random.randint(key, (total_obs,), 0, ROWS)
    rows_drawn = rows_drawn.at[0].set(0).at[OBS_DEV - 1].set(ROWS - 1)
    within_strip = jnp.arange(total_obs) % OBS_DEV
    obs_column = within_strip // (OBS_DEV // EASTWARD_CELLS)
    return (rows_drawn * EASTWARD_CELLS + obs_column).astype(jnp.int32)


def draw_observation_list(key, part):
    key = jax.random.fold_in(key, 12)
    key_strip, key_col, key_sub = jax.random.split(key, 3)
    list_shape = (NYC, NXC, OBS_PT)
    home_strip = (jnp.arange(NYC) // (ROWS // COARSE))[:, None, None]
    strip_pick = jnp.clip(home_strip + jax.random.randint(key_strip, list_shape, -2, 3), 0, NORTHWARD_CELLS // ROWS - 1)
    column = jnp.clip(COARSE * jnp.arange(NXC)[None, :, None] + jax.random.randint(key_col, list_shape, -COARSE, COARSE + 1), 0, EASTWARD_CELLS - 1)
    per_column = OBS_DEV // EASTWARD_CELLS
    picked = strip_pick * OBS_DEV + column * per_column + jax.random.randint(key_sub, list_shape, 0, per_column)
    picked = picked.at[0, 0, 0].set(0).at[NYC - 1, NXC - 1, 0].set(OBS_DEV * (NORTHWARD_CELLS // ROWS) - 1)
    return picked.astype(jnp.int32)


def draw_obs_count(key, part):
    key = jax.random.fold_in(key, 13)
    counts = jax.random.randint(key, (NYC, NXC), 1, OBS_PT + 1)
    return counts.at[0, 0].set(OBS_PT).at[0, 1].set(1).astype(jnp.int32)


def with_ends(drawn, own_key, smallest, top_value):
    spot = [jax.random.randint(jax.random.fold_in(own_key, axis), (), 0, length) for axis, length in enumerate(drawn.shape)]
    main_axis = drawn.shape.index(max(drawn.shape))
    neighbour = spot[:main_axis] + [(spot[main_axis] + 1) % drawn.shape[main_axis]] + spot[main_axis + 1:]
    return drawn.at[tuple(spot)].set(smallest).at[tuple(neighbour)].set(top_value)


def levels(stream_key, dims, shards, smallest, largest):
    factor_of = 1.0
    for axis_at, parts in shards:
        heights = jax.random.uniform(jax.random.fold_in(jax.random.fold_in(stream_key, 6), axis_at), (parts,), jnp.float32, smallest / len(shards), largest / len(shards))
        factor_of = factor_of * jnp.repeat(jnp.exp(heights), dims[axis_at] // parts).reshape((-1,) + (1,) * (len(dims) - 1 - axis_at))
    return factor_of


def noise(own_key, extent, width, limit, cuts=(), kind=jnp.bfloat16):
    result = width * jax.random.normal(own_key, extent, jnp.float32)
    if cuts:
        result = result * levels(own_key, extent, cuts, -0.22, 0.18)
    return jnp.clip(result, -limit, limit).astype(kind)


def setup_inputs(seed: int = 0) -> dict:
    key_list = jax.random.split(jax.random.key(seed), 11)
    trials_initial_dye = noise(key_list[0], (ENSEMBLE, LEV, NORTHWARD_CELLS, EASTWARD_CELLS), 1.0, 6.0, ((0, 4), (2, 32)), jnp.float32)
    diffusivity = jnp.clip(jnp.exp(jax.random.uniform(key_list[1], (LEV,), jnp.float32, math.log(0.02), math.log(0.2))), 0.02, 0.2)
    wet_mask = with_ends((jax.random.randint(key_list[2], (NORTHWARD_CELLS, EASTWARD_CELLS), 0, 8) < 7).astype(jnp.int32), jax.random.fold_in(key_list[2], 1), 0, 1)
    deeper_donor_tier = with_ends(jax.random.randint(key_list[3], (LEV, NORTHWARD_CELLS, EASTWARD_CELLS), 0, LEV - 1), jax.random.fold_in(key_list[3], 1), 0, (LEV - 1) - 1).astype(jnp.int32)
    shallower_tier_fraction = jnp.clip(1.0 * jax.random.uniform(key_list[4], (LEV, NORTHWARD_CELLS, EASTWARD_CELLS), jnp.float32) ** levels(key_list[4], (LEV, NORTHWARD_CELLS, EASTWARD_CELLS), ((1, 32),), -0.2, 0.2), 0.0, 1.0)
    obs_pos = draw_obs_pos(jax.random.fold_in(key_list[10], 71), 0)
    obs_value = noise(key_list[6], (OBS,), 1.0, 6.0, ((0, 32),), jnp.float32)
    obs_var = jnp.clip(jnp.exp(math.log(2.0) - 1.3862944 * jax.random.uniform(key_list[7], (OBS,), jnp.float32) ** levels(key_list[7], (OBS,), ((0, 32),), -0.2, 0.2)), 0.5, 2.0)
    observation_list = draw_observation_list(jax.random.fold_in(key_list[10], 71), 0)
    obs_count = draw_obs_count(jax.random.fold_in(key_list[10], 71), 0)
    return {"trials_initial_dye": trials_initial_dye, "diffusivity": diffusivity, "wet_mask": wet_mask, "deeper_donor_tier": deeper_donor_tier, "shallower_tier_fraction": shallower_tier_fraction, "obs_pos": obs_pos, "obs_value": obs_value, "obs_var": obs_var, "observation_list": observation_list, "obs_count": obs_count}


def depthwise_regridding(dye_map, deeper_donor_tier, shallower_tier_fraction):
    lower_value = jnp.zeros_like(dye_map)
    upper_value = jnp.zeros_like(dye_map)
    for level_no in range(LEV - 1):
        chosen = deeper_donor_tier == level_no
        lower_value = jnp.where(chosen, dye_map[..., level_no:level_no + 1, :, :], lower_value)
        upper_value = jnp.where(chosen, dye_map[..., level_no + 1:level_no + 2, :, :], upper_value)
    return (1.0 - shallower_tier_fraction) * lower_value + shallower_tier_fraction * upper_value

def point_weights(ens_obs, innovation, obs_var, obs_row, obs_col, point_row, point_col, live_slot):
    trial_tally = ens_obs.shape[0]
    dist_sq = (obs_row - point_row) ** 2 + (obs_col - point_col) ** 2
    taper_weight = jnp.where(live_slot, jnp.exp(-dist_sq / (2.0 * LOC * LOC)) / obs_var, 0.0)
    scaled = ens_obs * taper_weight
    gram_matrix = jnp.einsum('ikp,jkp->ijp', scaled, ens_obs, precision=lax.Precision.HIGHEST)
    identity_mat = jnp.eye(trial_tally, dtype=jnp.float32)[:, :, None]
    system = (trial_tally - 1.0) * identity_mat + gram_matrix
    frobenius = jnp.sqrt(lax.optimization_barrier(jnp.sum(system * system, axis=(0, 1))))
    root_iter = system / frobenius
    inverse_root = jnp.broadcast_to(identity_mat, system.shape)
    for turn_no in range(NS_ITERS):
        middle = 1.5 * identity_mat - 0.5 * jnp.einsum('ijp,jkp->ikp', inverse_root, root_iter, precision=lax.Precision.HIGHEST)
        root_iter = jnp.einsum('ijp,jkp->ikp', root_iter, middle, precision=lax.Precision.HIGHEST)
        inverse_root = jnp.einsum('ijp,jkp->ikp', middle, inverse_root, precision=lax.Precision.HIGHEST)
    drive_vec = jnp.einsum('ikp,kp->ip', scaled, innovation, precision=lax.Precision.HIGHEST)
    half_way = jnp.einsum('ijp,jp->ip', inverse_root, drive_vec, precision=lax.Precision.HIGHEST)
    mean_weight = jnp.einsum('ijp,jp->ip', inverse_root, half_way, precision=lax.Precision.HIGHEST) / frobenius
    return jnp.sqrt(trial_tally - 1.0) / jnp.sqrt(frobenius) * inverse_root + mean_weight[:, None, :]

def blend_weights(cell_block, padded_weights):
    span_cells = cell_block.shape[3]
    offset = (jnp.arange(span_cells, dtype=jnp.float32) - 0.5 * (span_cells - 1)) / span_cells
    coefficients = [jnp.maximum(-offset, 0.0), 1.0 - jnp.abs(offset), jnp.maximum(offset, 0.0)]
    rows_inner = padded_weights.shape[2] - 2
    cols_inner = padded_weights.shape[3] - 2
    blended = jnp.zeros_like(cell_block)
    for row_shift in range(3):
        for col_shift in range(3):
            tile_weights = padded_weights[:, :, row_shift:row_shift + rows_inner, col_shift:col_shift + cols_inner]
            product_term = jnp.einsum('ilarbc,ijab->jlarbc', cell_block, tile_weights, precision=lax.Precision.HIGHEST)
            blended = blended + coefficients[row_shift][:, None, None] * coefficients[col_shift] * product_term
    return blended - cell_block

def reference(trials_initial_dye, diffusivity, wet_mask, deeper_donor_tier, shallower_tier_fraction, obs_pos, obs_value, obs_var, observation_list, obs_count):
    trial_tally = trials_initial_dye.shape[0]
    ocean = wet_mask.astype(jnp.float32)
    diffusion_rate = diffusivity[:, None, None]

    def trial_propagated(trial_ocean_condition):
        dye_map = trial_ocean_condition
        for time_step in range(STEPS):
            padded = jnp.pad(dye_map, ((0, 0), (1, 1), (1, 1)))
            beside_all = padded[:, 2:, 1:-1] + padded[:, :-2, 1:-1] + padded[:, 1:-1, 2:] + padded[:, 1:-1, :-2]
            dye_map = ocean * (dye_map + diffusion_rate * (beside_all - 4.0 * dye_map))
        return depthwise_regridding(dye_map, deeper_donor_tier, shallower_tier_fraction)
    propagated_condition = lax.map(trial_propagated, trials_initial_dye)
    sample_centroid = lax.optimization_barrier(jnp.mean(propagated_condition, axis=0))
    trial_departure = propagated_condition - sample_centroid
    seaface_map = propagated_condition[:, 0].reshape(trial_tally, NORTHWARD_CELLS * EASTWARD_CELLS)
    strip_of = (jnp.arange(OBS) // OBS_DEV).astype(jnp.int32)
    flat_pos = strip_of * (ROWS * EASTWARD_CELLS) + obs_pos
    obs_ens = jnp.take(seaface_map, flat_pos, axis=1)
    obs_row = (strip_of * ROWS + obs_pos // EASTWARD_CELLS).astype(jnp.float32)
    obs_col = (obs_pos % EASTWARD_CELLS).astype(jnp.float32)
    obs_mean = lax.optimization_barrier(jnp.mean(obs_ens, axis=0))
    obs_pert = obs_ens - obs_mean
    innovation = obs_value - obs_mean
    half_cell = 0.5 * (COARSE - 1)

    def row_weights(coarse_row):
        sensor_ordinal = observation_list[coarse_row].T
        live_slot = jnp.arange(OBS_PT)[:, None] < obs_count[coarse_row][None, :]
        point_row = (COARSE * coarse_row).astype(jnp.float32) + half_cell + jnp.zeros((NXC,), jnp.float32)
        point_col = (COARSE * jnp.arange(NXC)).astype(jnp.float32) + half_cell
        return point_weights(jnp.take(obs_pert, sensor_ordinal, axis=1), jnp.take(innovation, sensor_ordinal), jnp.take(obs_var, sensor_ordinal), jnp.take(obs_row, sensor_ordinal), jnp.take(obs_col, sensor_ordinal), point_row, point_col, live_slot)
    weights_rows = lax.map(row_weights, jnp.arange(NYC))

    def apply_row(coarse_row):
        row_above = jnp.maximum(coarse_row - 1, 0)
        row_below = jnp.minimum(coarse_row + 1, NYC - 1)
        neighbours = jnp.stack([weights_rows[row_above], weights_rows[coarse_row], weights_rows[row_below]], axis=2)
        neighbours = jnp.concatenate([neighbours[..., :1], neighbours, neighbours[..., -1:]], axis=3)
        first_row = (coarse_row * COARSE).astype(jnp.int32)
        cell_block = lax.dynamic_slice_in_dim(trial_departure, first_row, COARSE, 2).reshape(trial_tally, LEV, 1, COARSE, NXC, COARSE)
        ocean_rows = lax.dynamic_slice_in_dim(ocean, first_row, COARSE, 0)
        return blend_weights(cell_block, neighbours).reshape(trial_tally, LEV, COARSE, EASTWARD_CELLS) * ocean_rows
    row_parts = lax.map(apply_row, jnp.arange(NYC))
    kalman_adjustment = jnp.transpose(row_parts, (1, 2, 0, 3, 4)).reshape(trial_tally, LEV, NORTHWARD_CELLS, EASTWARD_CELLS)
    return propagated_condition + kalman_adjustment
```

```python
import functools

import jax
import jax.numpy as jnp
from jax import lax
from jax.experimental import pallas as pl
from jax.experimental.pallas import tpu as pltpu
from jax.sharding import PartitionSpec as P

MESH = pl.DeviceIdType.MESH
F32 = jnp.float32
BF16 = jnp.bfloat16
STEPS = 4
NS_ITERS = 6
TASKS = 4
STRIPS = 32
GROUP = 4
SPAN = 276
LIMIT = 58 * 1024 * 1024


def iota(shape, dim):
    return lax.broadcasted_iota(jnp.int32, shape, dim)


def split(x):
    hi = x.astype(BF16)
    return hi, (x - hi.astype(F32)).astype(BF16)


def greet(peers):
    barrier = pltpu.get_barrier_semaphore()
    for peer in peers:
        pl.semaphore_signal(barrier, inc=1, device_id=peer, device_id_type=MESH)
    pl.semaphore_wait(barrier, len(peers))


def forecast_kernel(
    x, wet, donor, frac, rate, attr,
    w5, f1, e5, attr5,
    hal, whal, fs0, fs1, es,
    halo_s, halo_r, wet_s, wet_r, attr_s, attr_r, own, swap_s, swap_r, win_s, win_r, edge_s, edge_r,
):
    t = lax.axis_index("task")
    s = lax.axis_index("patch")
    strip = {d: lax.rem(s + d + STRIPS, STRIPS) for d in (-2, -1, 1, 2)}
    peer = {k: lax.rem(t + k, TASKS) for k in range(TASKS)}
    greet([(t, strip[d]) for d in (-2, -1, 1, 2)] + [(peer[k], s) for k in (1, 2, 3)])

    def send(src, dst, ss, rs, to):
        copy = pltpu.make_async_remote_copy(
            src_ref=src, dst_ref=dst, send_sem=ss, recv_sem=rs, device_id=to, device_id_type=MESH
        )
        copy.start()
        return copy

    wet_copies = []
    halo_copies = []
    for i, d in enumerate((-1, 1)):
        part = pl.ds(4 * i, 4)
        wet_copies.append(
            send(wet.at[part], whal.at[part], wet_s.at[i], wet_r.at[i], (t, strip[d]))
        )
    for c in range(4):
        members = pl.ds(4 * c, 4)
        for i, d in enumerate((-1, 1)):
            part = pl.ds(4 * i, 4)
            halo_copies.append(
                send(
                    x.at[members, :, part],
                    hal.at[members, :, part],
                    halo_s.at[2 * c + i],
                    halo_r.at[2 * c + i],
                    (t, strip[d]),
                )
            )
    attr_copies = [
        send(attr, attr5.at[2 - d], attr_s.at[i], attr_r.at[i], (t, strip[d]))
        for i, d in enumerate((-2, -1, 1, 2))
    ]
    own_attr = pltpu.make_async_copy(attr, attr5.at[2], own.at[0])
    own_attr.start()

    sub = iota((8, 1024), 0)
    col = iota((8, 1024), 1)
    lane = iota((8, 128), 1)
    below = jnp.where(s < STRIPS - 1, 1.0, 0.0)
    above = jnp.where(s > 0, 1.0, 0.0)
    inside = jnp.where(sub < 4, below, above)
    for copy in wet_copies:
        copy.wait()
    ocean = wet[...].astype(F32)
    ocean_halo = whal[...].astype(F32) * inside
    es[...] = jnp.zeros_like(es)

    def member(m, carry):
        levels = []
        for lev in range(4):
            here = x[m, lev]
            out = hal[m, lev] * inside
            k = rate[lev]
            for step in range(STEPS):
                east_h = jnp.where(col == 1023, 0.0, pltpu.roll(here, 1023, 1))
                west_h = jnp.where(col == 0, 0.0, pltpu.roll(here, 1, 1))
                down_h, down_o = pltpu.roll(here, 1, 0), pltpu.roll(out, 1, 0)
                up_h, up_o = pltpu.roll(here, 7, 0), pltpu.roll(out, 7, 0)
                beside = (
                    jnp.where(sub == 7, up_o, up_h)
                    + jnp.where(sub == 0, down_o, down_h)
                    + east_h
                    + west_h
                )
                new = ocean * (here + k * (beside - 4.0 * here))
                if step < STEPS - 1:
                    east_o = jnp.where(col == 1023, 0.0, pltpu.roll(out, 1023, 1))
                    west_o = jnp.where(col == 0, 0.0, pltpu.roll(out, 1, 1))
                    beside = (
                        jnp.where(sub == 7, up_h, up_o)
                        + jnp.where(sub == 0, down_h, down_o)
                        + east_o
                        + west_o
                    )
                    out = ocean_halo * (out + k * (beside - 4.0 * out))
                here = new
            levels.append(here)
        for lev in range(4):
            tier = donor[lev]
            low = jnp.where(tier == 0, levels[0], jnp.where(tier == 1, levels[1], levels[2]))
            high = jnp.where(tier == 0, levels[1], jnp.where(tier == 1, levels[2], levels[3]))
            share = frac[lev]
            result = (1.0 - share) * low + share * high
            if lev:
                fs1[m, lev - 1] = result
            else:
                fs0[m] = result
                for k in range(TASKS):
                    right = result[:, 256 * (k + 1) % 1024 : 256 * (k + 1) % 1024 + 128]
                    left = result[:, (256 * k - 128) % 1024 : (256 * k - 128) % 1024 + 128]
                    rim = pltpu.roll(jnp.where(lane >= 124, left, right), m * 8 + 4, 1)
                    es[k] = jnp.where(lane // 8 == m, rim, es[k])
        return carry

    for c in range(4):
        halo_copies[2 * c].wait_recv()
        halo_copies[2 * c + 1].wait_recv()
        lax.fori_loop(4 * c, 4 * c + 4, member, 0)

    mine = pl.ds(pl.multiple_of(16 * t, 16), 16)
    local = []
    swaps = {}
    here_cols = pl.ds(pl.multiple_of(256 * t, 256), 256)
    for n, (src, dst) in enumerate(
        [
            (fs0.at[:, :, here_cols], w5.at[2, mine]),
            (es.at[t], e5.at[2, t]),
            (fs1.at[:, :, :, here_cols], f1.at[mine]),
        ]
    ):
        copy = pltpu.make_async_copy(src, dst, own.at[1 + n])
        copy.start()
        local.append(copy)
    for n in range(3):
        for k in (1, 2, 3):
            to = peer[k]
            cols = pl.ds(pl.multiple_of(256 * to, 256), 256)
            src, dst = (
                (fs0.at[:, :, cols], w5.at[2, mine]),
                (es.at[to], e5.at[2, t]),
                (fs1.at[:, :, :, cols], f1.at[mine]),
            )[n]
            i = 3 * n + k - 1
            swaps[n, k] = send(src, dst, swap_s.at[i], swap_r.at[i], (to, s))

    windows = []
    for k in range(TASKS):
        if k:
            swaps[0, k].wait_recv()
        else:
            local[0].wait()
        src = lax.rem(t - k + TASKS, TASKS)
        part = pl.ds(pl.multiple_of(16 * src, 16), 16)
        for i, d in enumerate((-2, 2, -1, 1)):
            n = 4 * k + i
            windows.append(
                send(w5.at[2, part], w5.at[2 - d, part], win_s.at[n], win_r.at[n], (t, strip[d]))
            )
    local[1].wait()
    for k in (1, 2, 3):
        swaps[1, k].wait_recv()
    for i, d in enumerate((-2, 2, -1, 1)):
        windows.append(
            send(e5.at[2], e5.at[2 - d], edge_s.at[i], edge_r.at[i], (t, strip[d]))
        )
    for copy in windows + attr_copies:
        copy.wait()
    own_attr.wait()
    local[2].wait()
    for (n, k), copy in swaps.items():
        copy.wait_send()
        if n == 2:
            copy.wait_recv()
    for copy in halo_copies:
        copy.wait_send()


def forecast(x, wet, donor, frac, rate, attr):
    dma = pltpu.SemaphoreType.DMA
    vmem = pl.BlockSpec(memory_space=pltpu.VMEM)
    anywhere = pl.BlockSpec(memory_space=pl.ANY)
    return pl.pallas_call(
        forecast_kernel,
        out_shape=[
            jax.ShapeDtypeStruct((5, 64, 8, 256), F32),
            jax.ShapeDtypeStruct((64, 3, 8, 256), F32),
            jax.ShapeDtypeStruct((5, 4, 8, 128), F32),
            jax.ShapeDtypeStruct((5, 3, 32, 128), F32),
        ],
        in_specs=[vmem, vmem, vmem, vmem, pl.BlockSpec(memory_space=pltpu.SMEM), vmem],
        out_specs=[anywhere] * 4,
        scratch_shapes=[
            pltpu.VMEM((16, 4, 8, 1024), F32),
            pltpu.VMEM((8, 1024), jnp.int32),
            pltpu.VMEM((16, 8, 1024), F32),
            pltpu.VMEM((16, 3, 8, 1024), F32),
            pltpu.VMEM((4, 8, 128), F32),
            dma((8,)), dma((8,)), dma((2,)), dma((2,)), dma((4,)), dma((4,)),
            dma((4,)), dma((9,)), dma((9,)), dma((16,)), dma((16,)), dma((4,)), dma((4,)),
        ],
        compiler_params=pltpu.CompilerParams(
            collective_id=0, has_side_effects=True, vmem_limit_bytes=LIMIT
        ),
    )(x, wet, donor, frac, rate, attr)


def spread(x, shift):
    lane = iota(x.shape, 1)
    return jnp.where(
        lane < 64, pltpu.roll(x, (127 - shift) % 128, 1), pltpu.roll(x, 63 - shift, 1)
    )


def doubled(x):
    hi, lo = split(x)
    left = iota(x.shape, 1) < 64
    zero = jnp.zeros((64, 128), BF16)

    def diagonal(y):
        y = y.astype(F32)
        return jnp.concatenate(
            [jnp.where(left, y, 0.0), jnp.where(left, 0.0, y)], axis=0
        ).astype(BF16)

    hi, lo = diagonal(hi), diagonal(lo)
    zero = jnp.zeros((128, 128), BF16)
    return jnp.concatenate(
        [jnp.concatenate([hi, lo], axis=1), jnp.concatenate([hi, zero], axis=1)], axis=0
    )


def times(x, weights):
    hi, lo = split(x)
    product = jnp.dot(
        jnp.concatenate([hi, lo], axis=1), weights, preferred_element_type=F32
    )
    return product[:, :128] + product[:, 128:]


def weights_kernel(w5, e5, attr, code, out, cols, rim, mean, picked, base, taper, force, system, drive):
    lane = iota((8, 128), 1)
    sub = iota((8, 128), 0)

    def place(st, carry):
        for src in range(TASKS):
            tile = e5[st, src]
            for m in range(16):
                rim[16 * src + m] = pltpu.roll(tile, (128 - 8 * m) % 128, 1) if m else tile
        rows = pl.ds(pl.multiple_of(8 * st, 8), 8)
        means, rim_means = [], []
        for r in range(8):
            whole = w5[st, :, r, :]
            mu = jnp.sum(whole, axis=0, keepdims=True) * (1.0 / 64)
            dev = whole - mu
            cols[4:260, st, r, :] = jnp.concatenate([dev, dev], axis=0).T
            means.append(mu)
            whole = rim[:, r, :]
            mu = jnp.sum(whole, axis=0, keepdims=True) * (1.0 / 64)
            dev = whole - mu
            turned = jnp.concatenate([dev, dev], axis=0).T
            cols[0:4, st, r, :] = turned[0:4]
            cols[260:264, st, r, :] = turned[4:8]
            rim_means.append(mu)
        mean[rows, 0:256] = jnp.concatenate(means, axis=0)
        mean[rows, 256:384] = jnp.concatenate(rim_means, axis=0)
        return carry

    lax.fori_loop(0, 5, place, 0)

    spot = iota((384, 128), 0)
    coarse = iota((384, 128), 1)
    lane_of = iota((40, 384), 1)
    known = jnp.where(lane_of < 264, mean[...], 0.0)
    for q in range(4):
        want = jnp.where(
            coarse == 0, 256 + q, jnp.where(coarse == 65, 260 + q, 4 * coarse - 4 + q)
        )
        picked[q] = jnp.dot(
            known,
            jnp.where((spot == want) & (coarse < 66), 1.0, 0.0),
            precision=lax.Precision.HIGHEST,
            preferred_element_type=F32,
        )
    for slot in range(32):
        base[slot] = jnp.broadcast_to(code[slot : slot + 1, :], (8, 128)) - sub

    point_row = jnp.where(lane < 64, 1.5, 5.5)
    height = sub.astype(F32)
    taper[45] = jnp.zeros((8, 128), F32)

    def weigh(st, carry):
        for cr in range(9):
            q, shift = (cr - 4) % 4, (cr - 4) // 4
            row = spread(attr[st, 0, 8 * q : 8 * q + 8, :], shift)
            value = spread(attr[st, 1, 8 * q : 8 * q + 8, :], shift)
            var = spread(attr[st, 2, 8 * q : 8 * q + 8, :], shift)
            tile = (st * 9 + cr) * 8
            count = jnp.zeros((8, 128), F32)
            for slot in range(32):
                count = count + jnp.where(base[slot] == tile, 1.0, 0.0)
            apart = row + (8.0 * (st - 2).astype(F32)) - point_row
            dist = apart * apart + (cr - 5.5) ** 2
            weight = count * jnp.exp(dist * (-1.0 / 1152.0)) / var
            pull = weight * value
            total = jnp.zeros((8, 128), F32)
            pulled = jnp.zeros((8, 128), F32)
            for k in range(8):
                hit = row[k : k + 1] == height
                total = total + jnp.where(hit, weight[k : k + 1], 0.0)
                pulled = pulled + jnp.where(hit, pull[k : k + 1], 0.0)
            centre = spread(picked[q, pl.ds(pl.multiple_of(8 * st, 8), 8), :], shift)
            taper[cr * 5 + st] = total
            force[cr * 5 + st] = pulled - total * centre
        return carry

    lax.fori_loop(0, 5, weigh, 0)

    tall_lane = iota((368, 128), 1)
    eye = jnp.where(iota((64, 128), 0) == iota((64, 128), 1) % 64, 1.0, 0.0)

    def gram(b, carry):
        index = jnp.where(lane < 64, b, 64 + b)
        near = cols[pl.ds(4 * b, 10)].reshape(400, 128)[:368]
        spread_taper = jnp.concatenate(
            [jnp.take_along_axis(taper[k], index, axis=1) for k in range(46)], axis=0
        )
        spread_force = jnp.concatenate(
            [jnp.take_along_axis(force[k], index, axis=1) for k in range(45)], axis=0
        )
        s_hi, s_lo = split(near * spread_taper)
        n_hi = near.astype(BF16).astype(F32)
        both = jnp.where(tall_lane < 64, n_hi, near - n_hi).astype(BF16)
        product = lax.dot_general(
            both,
            jnp.concatenate([s_hi, s_lo], axis=1),
            (((0,), (0,)), ((), ())),
            preferred_element_type=F32,
        )
        product = product[:64] + product[64:]
        system[b] = product[:, :128] + product[:, 128:] + 63.0 * eye
        drive[b] = jnp.broadcast_to(
            jnp.sum(near[:360] * spread_force, axis=0, keepdims=True), (8, 128)
        )
        return carry

    lax.fori_loop(0, 64, gram, 0)

    half = iota((64, 128), 1) < 64

    def solve(n, carry):
        pairs = [n * GROUP + k for k in range(GROUP)]
        roots, inverses, norms = [], [], []
        for b in pairs:
            x = system[b]
            squares = jnp.sum(x * x, axis=0, keepdims=True)
            left = iota((1, 128), 1) < 64
            one = jnp.sum(jnp.where(left, squares, 0.0), axis=1, keepdims=True)
            two = jnp.sum(jnp.where(left, 0.0, squares), axis=1, keepdims=True)
            norm = jnp.sqrt(jnp.where(left, one, two))
            norms.append(norm)
            roots.append(x / norm)
            inverses.append(None)
        for turn in range(NS_ITERS):
            middles = []
            for k in range(GROUP):
                if turn == 0:
                    middles.append(1.5 * eye - 0.5 * roots[k])
                else:
                    middles.append(1.5 * eye - 0.5 * times(inverses[k], doubled(roots[k])))
            for k in range(GROUP):
                weights = doubled(middles[k])
                if turn == 0:
                    inverses[k] = middles[k]
                    roots[k] = times(roots[k], weights)
                elif turn < NS_ITERS - 1:
                    both = times(jnp.concatenate([roots[k], inverses[k]], axis=0), weights)
                    roots[k], inverses[k] = both[:64], both[64:]
                else:
                    inverses[k] = times(inverses[k], weights)
        finals = []
        for k, b in enumerate(pairs):
            weights = doubled(inverses[k])
            drift = times(times(drive[b], weights), weights)[:1] / norms[k]
            on_diagonal = eye * drift
            one = jnp.sum(jnp.where(half, on_diagonal, 0.0), axis=1, keepdims=True)
            two = jnp.sum(jnp.where(half, 0.0, on_diagonal), axis=1, keepdims=True)
            finals.append(
                jnp.sqrt(63.0 / norms[k]) * inverses[k] + jnp.where(half, one, two)
            )
        for k in range(0, GROUP, 2):
            g = n * (GROUP // 2) + k // 2
            out[0, g] = jnp.where(half, finals[k], pltpu.roll(finals[k + 1], 64, 1))
            out[1, g] = jnp.where(half, pltpu.roll(finals[k], 64, 1), finals[k + 1])
        return carry

    lax.fori_loop(0, 64 // GROUP, solve, 0)


def point_weights(w5, e5, attr5, code):
    vmem = pl.BlockSpec(memory_space=pltpu.VMEM)
    return pl.pallas_call(
        weights_kernel,
        out_shape=jax.ShapeDtypeStruct((2, 32, 64, 128), F32),
        in_specs=[vmem] * 4,
        out_specs=vmem,
        scratch_shapes=[
            pltpu.VMEM((264, 5, 8, 128), F32),
            pltpu.VMEM((64, 8, 128), F32),
            pltpu.VMEM((40, 384), F32),
            pltpu.VMEM((4, 40, 128), F32),
            pltpu.VMEM((32, 8, 128), jnp.int32),
            pltpu.VMEM((46, 8, 128), F32),
            pltpu.VMEM((45, 8, 128), F32),
            pltpu.VMEM((64, 64, 128), F32),
            pltpu.VMEM((64, 8, 128), F32),
        ],
        compiler_params=pltpu.CompilerParams(vmem_limit_bytes=LIMIT),
    )(w5, e5, attr5, code)


def hat(x):
    return jnp.maximum(1.0 - jnp.abs(x - 1.5) * 0.25, 0.0)


def analysis_kernel(
    weights, w5, f1, wet,
    out,
    every, f0, turned, total, result,
    own, side_s, side_r, row_s, row_r, corner_s, corner_r, back_s, back_r,
):
    t = lax.axis_index("task")
    s = lax.axis_index("patch")
    up, down = lax.rem(s + STRIPS - 1, STRIPS), lax.rem(s + 1, STRIPS)
    peer = {k: lax.rem(t + k, TASKS) for k in range(TASKS)}
    right, left = peer[1], peer[3]
    load = pltpu.make_async_copy(w5.at[2], f0, own.at[0])
    load.start()
    greet(
        [(peer[k], s) for k in (1, 2, 3)]
        + [(t, up), (t, down)]
        + [(x, y) for x in (right, left) for y in (up, down)]
    )

    def send(src, dst, ss, rs, to):
        copy = pltpu.make_async_remote_copy(
            src_ref=src, dst_ref=dst, send_sem=ss, recv_sem=rs, device_id=to, device_id_type=MESH
        )
        copy.start()
        return copy

    copies = []
    for i, (to, mine, there) in enumerate([(right, 31, 0), (left, 0, 33)]):
        for a in range(2):
            copies.append(
                send(
                    weights.at[a, mine], every.at[1 + a, there],
                    side_s.at[2 * i + a], side_r.at[2 * i + a], (to, s),
                )
            )
            copies.append(
                send(
                    weights.at[a, mine], every.at[3 - 3 * a, there],
                    corner_s.at[2 * i + a], corner_r.at[2 * i + a], (to, (up, down)[a]),
                )
            )
    for a in range(2):
        copies.append(
            send(
                weights.at[a], every.at[3 - 3 * a, pl.ds(1, 32)],
                row_s.at[a], row_r.at[a], (t, (up, down)[a]),
            )
        )

    total[...] = jnp.zeros_like(total)
    load.wait()
    lane_wide = iota((256, 128), 1) < 64
    cols = pl.ds(pl.multiple_of(256 * t, 256), 256)

    def field(lev, r):
        return f0[:, r, :] if lev == 0 else f1[:, lev - 1, r, :]

    def deviation(lev, r):
        whole = field(lev, r)
        return whole - jnp.sum(whole, axis=0, keepdims=True) * (1.0 / 64)

    for lev in range(4):
        for r in range(8):
            dev = deviation(lev, r)
            both = jnp.concatenate([dev, dev], axis=0).T
            high = both.astype(BF16).astype(F32)
            turned[10:266, r // 2, 4 * (r % 2) + lev, :] = jnp.where(
                lane_wide, high, both - high
            )

    lane = iota((8, 128), 1)
    sub = iota((8, 128), 0)
    second = jnp.where(lane < 64, 0.0, 4.0)
    top = jnp.where(s == 0, 1.0, 0.0)
    bottom = jnp.where(s == STRIPS - 1, 1.0, 0.0)

    def row_share(a, k):
        r = (2 * k + sub // 4).astype(F32)
        if a == -1:
            return hat(r + 4.0) * (1.0 - top)
        if a == 0:
            return hat(r) + hat(r + 4.0) * top
        if a == 1:
            return hat(r - 4.0) + hat(r - 8.0) * bottom
        return hat(r - 8.0) * (1.0 - bottom)

    def col_share(g):
        first = jnp.where((g == 0) & (t == 0), 1.0, 0.0)
        last = jnp.where((g == 31) & (t == TASKS - 1), 1.0, 0.0)
        alive = jnp.where(
            ((g == -1) & (t == 0)) | ((g == 32) & (t == TASKS - 1)), 0.0, 1.0
        )
        shares = []
        for c in range(12):
            x = (c - 2.0) - second
            share = hat(x)
            if c in (2, 3):
                share = share + jnp.where(lane < 64, hat(x + 4.0), 0.0) * first
            if c in (8, 9):
                share = share + jnp.where(lane < 64, 0.0, hat(x - 4.0)) * last
            shares.append(share * alive)
        return shares

    def paired(x):
        hi, lo = split(x)
        zero = jnp.zeros((64, 128), BF16)
        return jnp.concatenate(
            [jnp.concatenate([hi, lo], axis=1), jnp.concatenate([hi, zero], axis=1)], axis=0
        )

    def add(g, a, operand, first, count, shares):
        rows = turned[pl.ds(8 * g + 8, 12), first : first + count]
        rows = rows.reshape(12 * count * 8, 128).astype(BF16)
        product = jnp.dot(rows, paired(operand), preferred_element_type=F32)
        product = (product[:, :128] + product[:, 128:]).reshape(12, count, 8, 128)
        parts = []
        for c in range(12):
            parts.append(
                jnp.stack(
                    [product[c, k] * row_share(a, first + k) * shares[c] for k in range(count)]
                )
            )
        total[pl.ds(8 * g + 8, 12), first : first + count] += jnp.stack(parts)

    def inner(g, carry):
        shares = col_share(g)
        add(g, 0, weights[0, g], 0, 3, shares)
        add(g, 1, weights[1, g], 1, 3, shares)
        return carry

    lax.fori_loop(0, 32, inner, 0)

    for copy in copies:
        copy.wait()

    for g in (-1, 32):
        shares = col_share(g)
        add(g, 0, every[1, g + 1], 0, 3, shares)
        add(g, 1, every[2, g + 1], 1, 3, shares)

    def outer(n, carry):
        g = n - 1
        shares = col_share(g)
        add(g, -1, every[0, n], 0, 1, shares)
        add(g, 2, every[3, n], 3, 1, shares)
        return carry

    lax.fori_loop(0, 34, outer, 0)

    for r in range(8):
        ocean = wet[r : r + 1, cols].astype(F32)
        for lev in range(4):
            back = total[10:266, r // 2, 4 * (r % 2) + lev, :].T
            blended = back[:64] + back[64:]
            result[:, lev, r, :] = field(lev, r) + ocean * (blended - deviation(lev, r))

    mine = pl.ds(pl.multiple_of(16 * t, 16), 16)
    keep = pltpu.make_async_copy(result.at[mine], out.at[:, :, :, cols], own.at[1])
    keep.start()
    copies = []
    for k in (1, 2, 3):
        theirs = pl.ds(pl.multiple_of(16 * peer[k], 16), 16)
        copies.append(
            send(
                result.at[theirs], out.at[:, :, :, cols],
                back_s.at[k - 1], back_r.at[k - 1], (peer[k], s),
            )
        )
    for copy in copies:
        copy.wait()
    keep.wait()


def analysed(weights, w5, f1, wet):
    dma = pltpu.SemaphoreType.DMA
    vmem = pl.BlockSpec(memory_space=pltpu.VMEM)
    anywhere = pl.BlockSpec(memory_space=pl.ANY)
    return pl.pallas_call(
        analysis_kernel,
        out_shape=jax.ShapeDtypeStruct((16, 4, 8, 1024), F32),
        in_specs=[vmem, anywhere, vmem, vmem],
        out_specs=anywhere,
        scratch_shapes=[
            pltpu.VMEM((4, 34, 64, 128), F32),
            pltpu.VMEM((64, 8, 256), F32),
            pltpu.VMEM((SPAN, 4, 8, 128), F32),
            pltpu.VMEM((SPAN, 4, 8, 128), F32),
            pltpu.VMEM((64, 4, 8, 256), F32),
            dma((2,)), dma((4,)), dma((4,)), dma((2,)), dma((2,)), dma((4,)), dma((4,)),
            dma((3,)), dma((3,)),
        ],
        compiler_params=pltpu.CompilerParams(
            collective_id=1, has_side_effects=True, vmem_limit_bytes=LIMIT
        ),
    )(weights, w5, f1, wet)


def body(
    trials_initial_dye,
    diffusivity,
    wet_mask,
    deeper_donor_tier,
    shallower_tier_fraction,
    obs_pos,
    obs_value,
    obs_var,
    observation_list,
    obs_count,
):
    t = lax.axis_index("task")
    s = lax.axis_index("patch")
    facts = jnp.stack([(obs_pos // 1024).astype(F32), obs_value, obs_var])
    facts = facts.reshape(3, 256, 32).transpose(0, 2, 1)
    facts = jnp.pad(facts, ((0, 0), (0, 0), (1, 127)), constant_values=1.0)
    attr = lax.dynamic_slice_in_dim(facts, 64 * t, 128, 2)
    w5, f1, e5, attr5 = forecast(
        trials_initial_dye,
        wet_mask,
        deeper_donor_tier,
        shallower_tier_fraction,
        diffusivity,
        attr,
    )
    rel_strip = observation_list // 8192 - (s - 2)
    rel_col = observation_list % 8192 // 8 - (
        256 * t + 4 * jnp.arange(64, dtype=jnp.int32)[None, :, None] - 4
    )
    code = (rel_strip * 9 + rel_col) * 8 + observation_list % 8
    live = jnp.arange(32, dtype=jnp.int32)[None, None, :] < obs_count[:, :, None]
    code = jnp.where(live, code, -100000).reshape(128, 32).T
    weights = point_weights(w5, e5, attr5, code)
    return analysed(weights, w5, f1, wet_mask)


def solution(mesh):
    return jax.shard_map(
        body,
        mesh=mesh,
        in_specs=(
            P("task", None, "patch", None),
            P(),
            P("patch", None),
            P(None, "patch", None),
            P(None, "patch", None),
            P("patch"),
            P("patch"),
            P("patch"),
            P("patch", "task", None),
            P("patch", "task"),
        ),
        out_specs=P("task", None, "patch", None),
        check_vma=False,
    )
```

```python
import functools

import jax
import jax.numpy as jnp
from jax import lax
from jax.experimental import pallas as pl
from jax.experimental.pallas import tpu as pltpu
from jax.sharding import PartitionSpec as P

MESH = pl.DeviceIdType.MESH
F32 = jnp.float32
BF16 = jnp.bfloat16
STEPS = 4
NS_ITERS = 6
TASKS = 4
STRIPS = 32
GROUP = 8
SPAN = 276
LIMIT = 58 * 1024 * 1024


def iota(shape, dim):
    return lax.broadcasted_iota(jnp.int32, shape, dim)


def split(x):
    hi = x.astype(BF16)
    return hi, (x - hi.astype(F32)).astype(BF16)


def greet(peers):
    barrier = pltpu.get_barrier_semaphore()
    for peer in peers:
        pl.semaphore_signal(barrier, inc=1, device_id=peer, device_id_type=MESH)
    pl.semaphore_wait(barrier, len(peers))


def sender(src, dst, ss, rs, to):
    return pltpu.make_async_remote_copy(
        src_ref=src, dst_ref=dst, send_sem=ss, recv_sem=rs, device_id=to, device_id_type=MESH
    )


def forecast_kernel(
    x, wet, donor, frac, rate, pos, value, var,
    w5, fs1, e5, attr5,
    hal, whal, fs0, es, attr,
    halo_s, halo_r, wet_s, wet_r, attr_s, attr_r, own, swap_s, swap_r, rim_s, rim_r,
    win_s, win_r, edge_s, edge_r,
):
    t = lax.axis_index("task")
    s = lax.axis_index("patch")
    strip = {d: lax.rem(s + d + STRIPS, STRIPS) for d in (-2, -1, 1, 2)}
    peer = {k: lax.rem(t + k, TASKS) for k in range(TASKS)}
    way = 1 - 2 * lax.rem(s, 2)
    mate = s + way
    second = lax.rem(s + 2 * way + STRIPS, STRIPS)
    other = lax.rem(s - way + STRIPS, STRIPS)
    greet([(t, strip[d]) for d in (-2, -1, 1, 2)] + [(peer[k], s) for k in (1, 2, 3)])

    def send(src, dst, ss, rs, to):
        copy = sender(src, dst, ss, rs, to)
        copy.start()
        return copy

    wet_copies = []
    halo_copies = []
    for i, d in enumerate((-1, 1)):
        part = pl.ds(4 * i, 4)
        wet_copies.append(
            send(wet.at[part], whal.at[part], wet_s.at[i], wet_r.at[i], (t, strip[d]))
        )
    for c in range(4):
        members = pl.ds(4 * c, 4)
        for i, d in enumerate((-1, 1)):
            part = pl.ds(4 * i, 4)
            halo_copies.append(
                send(
                    x.at[members, :, part],
                    hal.at[members, :, part],
                    halo_s.at[2 * c + i],
                    halo_r.at[2 * c + i],
                    (t, strip[d]),
                )
            )

    facts = jnp.concatenate(
        [(pos[...] // 1024).astype(F32).T, value[...].T, var[...].T], axis=0
    )
    spot = iota((64, 128), 0)
    coarse = iota((64, 128), 1) - 1
    gathered = jnp.zeros((96, 128), F32)
    for m in range(4):
        taken = (spot == (coarse + 4) // 4 - 1 + 16 * t) & ((coarse + 4) % 4 == m)
        rows = jnp.concatenate([facts[128 * i + 32 * m : 128 * i + 32 * m + 32] for i in range(3)])
        gathered = gathered + jnp.dot(
            rows,
            jnp.where(taken, 1.0, 0.0),
            precision=lax.Precision.HIGHEST,
            preferred_element_type=F32,
        )
    lane96 = iota((32, 128), 1)
    known = (lane96 - 1 + 64 * t >= 0) & (lane96 - 1 + 64 * t < 256)
    attr[0] = gathered[0:32]
    attr[1] = gathered[32:64]
    attr[2] = jnp.where(known, gathered[64:96], 1.0)
    own_attr = pltpu.make_async_copy(attr, attr5.at[2], own.at[0])
    own_attr.start()

    sub = iota((8, 1024), 0)
    col = iota((8, 1024), 1)
    lane = iota((8, 128), 1)
    below = jnp.where(s < STRIPS - 1, 1.0, 0.0)
    above = jnp.where(s > 0, 1.0, 0.0)
    inside = jnp.where(sub < 4, below, above)
    for copy in wet_copies:
        copy.wait()
    ocean = wet[...].astype(F32)
    ocean_halo = whal[...].astype(F32) * inside
    es[...] = jnp.zeros_like(es)

    def member(m, carry):
        levels = []
        for lev in range(4):
            here = x[m, lev]
            out = hal[m, lev] * inside
            k = rate[lev]
            for step in range(STEPS):
                east_h = jnp.where(col == 1023, 0.0, pltpu.roll(here, 1023, 1))
                west_h = jnp.where(col == 0, 0.0, pltpu.roll(here, 1, 1))
                down_h, down_o = pltpu.roll(here, 1, 0), pltpu.roll(out, 1, 0)
                up_h, up_o = pltpu.roll(here, 7, 0), pltpu.roll(out, 7, 0)
                beside = (
                    jnp.where(sub == 7, up_o, up_h)
                    + jnp.where(sub == 0, down_o, down_h)
                    + east_h
                    + west_h
                )
                new = ocean * (here + k * (beside - 4.0 * here))
                if step < STEPS - 1:
                    east_o = jnp.where(col == 1023, 0.0, pltpu.roll(out, 1023, 1))
                    west_o = jnp.where(col == 0, 0.0, pltpu.roll(out, 1, 1))
                    beside = (
                        jnp.where(sub == 7, up_h, up_o)
                        + jnp.where(sub == 0, down_h, down_o)
                        + east_o
                        + west_o
                    )
                    out = ocean_halo * (out + k * (beside - 4.0 * out))
                here = new
            levels.append(here)
        for lev in range(4):
            tier = donor[lev]
            low = jnp.where(tier == 0, levels[0], jnp.where(tier == 1, levels[1], levels[2]))
            high = jnp.where(tier == 0, levels[1], jnp.where(tier == 1, levels[2], levels[3]))
            share = frac[lev]
            result = (1.0 - share) * low + share * high
            if lev:
                fs1[m, lev - 1] = result
            else:
                fs0[m] = result
                for k in range(TASKS):
                    right = result[:, 256 * (k + 1) % 1024 : 256 * (k + 1) % 1024 + 128]
                    left = result[:, (256 * k - 128) % 1024 : (256 * k - 128) % 1024 + 128]
                    rim = pltpu.roll(jnp.where(lane >= 124, left, right), m * 8 + 4, 1)
                    es[k] = jnp.where(lane // 8 == m, rim, es[k])
        return carry

    here_cols = pl.ds(pl.multiple_of(256 * t, 256), 256)
    local = []
    swaps = {}
    windows = {}

    def block(src, c):
        return pl.ds(pl.multiple_of(16 * src + 4 * c, 4), 4)

    def exchange(c):
        chunk = pl.ds(4 * c, 4)
        copy = pltpu.make_async_copy(
            fs0.at[chunk, :, here_cols], w5.at[2, block(t, c)], own.at[1 + c]
        )
        copy.start()
        local.append(copy)
        for k in (1, 2, 3):
            to = peer[k]
            cols = pl.ds(pl.multiple_of(256 * to, 256), 256)
            i = 3 * c + k - 1
            swaps[c, k] = send(
                fs0.at[chunk, :, cols], w5.at[2, block(t, c)], swap_s.at[i], swap_r.at[i], (to, s)
            )

    def forward(c):
        for k in range(TASKS):
            src = lax.rem(t - k + TASKS, TASKS)
            part = block(src, c)
            if k:
                swaps[c, k].wait_recv()
                held = w5.at[2, part]
            else:
                held = fs0.at[pl.ds(4 * c, 4), :, here_cols]
            for j, (to, slot) in enumerate(
                ((other, 2 + way), (second, 2 - 2 * way), (mate, 2 - way))
            ):
                i = 16 * j + 4 * c + k
                windows[j, c, k] = send(
                    held, w5.at[slot, part], win_s.at[i], win_r.at[i], (t, to)
                )

    def relay(c):
        for k in range(TASKS):
            src = lax.rem(t - k + TASKS, TASKS)
            part = block(src, c)
            windows[0, c, k].wait_recv()
            i = 48 + 4 * c + k
            windows[3, c, k] = send(
                w5.at[2 - way, part], w5.at[2 - 2 * way, part],
                win_s.at[i], win_r.at[i], (t, mate),
            )

    for c in range(4):
        halo_copies[2 * c].wait_recv()
        halo_copies[2 * c + 1].wait_recv()
        lax.fori_loop(4 * c, 4 * c + 4, member, 0)
        exchange(c)
        if c == 3:
            rims = []
            for k in (1, 2, 3):
                rims.append(
                    send(
                        es.at[peer[k]], e5.at[2, t], rim_s.at[k - 1], rim_r.at[k - 1], (peer[k], s)
                    )
                )
            own_rim = pltpu.make_async_copy(es.at[t], e5.at[2, t], own.at[5])
            own_rim.start()
        if c:
            forward(c - 1)
    forward(3)
    attr_copies = [
        send(attr, attr5.at[2 - d], attr_s.at[i], attr_r.at[i], (t, strip[d]))
        for i, d in enumerate((-2, -1, 1, 2))
    ]
    own_rim.wait()
    for copy in rims:
        copy.wait_recv()
    edges = [
        send(e5.at[2], e5.at[2 - d], edge_s.at[i], edge_r.at[i], (t, strip[d]))
        for i, d in enumerate((-2, -1, 1, 2))
    ]
    for c in range(4):
        relay(c)
    for copy in halo_copies + rims:
        copy.wait_send()
    for copy in swaps.values():
        copy.wait_send()
    for copy in local:
        copy.wait()
    for (j, c, k), copy in windows.items():
        copy.wait_send()
        if j:
            copy.wait_recv()
    for copy in attr_copies + edges:
        copy.wait()
    own_attr.wait()


def forecast(x, wet, donor, frac, rate, pos, value, var):
    dma = pltpu.SemaphoreType.DMA
    vmem = pl.BlockSpec(memory_space=pltpu.VMEM)
    anywhere = pl.BlockSpec(memory_space=pl.ANY)
    return pl.pallas_call(
        forecast_kernel,
        out_shape=[
            jax.ShapeDtypeStruct((5, 64, 8, 256), F32),
            jax.ShapeDtypeStruct((16, 3, 8, 1024), F32),
            jax.ShapeDtypeStruct((5, 4, 8, 128), F32),
            jax.ShapeDtypeStruct((5, 3, 32, 128), F32),
        ],
        in_specs=[vmem] * 4 + [pl.BlockSpec(memory_space=pltpu.SMEM)] + [vmem] * 3,
        out_specs=[anywhere, vmem, anywhere, anywhere],
        scratch_shapes=[
            pltpu.VMEM((16, 4, 8, 1024), F32),
            pltpu.VMEM((8, 1024), jnp.int32),
            pltpu.VMEM((16, 8, 1024), F32),
            pltpu.VMEM((4, 8, 128), F32),
            pltpu.VMEM((3, 32, 128), F32),
            dma((8,)), dma((8,)), dma((2,)), dma((2,)), dma((4,)), dma((4,)),
            dma((6,)), dma((12,)), dma((12,)), dma((3,)), dma((3,)),
            dma((64,)), dma((64,)), dma((4,)), dma((4,)),
        ],
        compiler_params=pltpu.CompilerParams(
            collective_id=0, has_side_effects=True, vmem_limit_bytes=LIMIT
        ),
    )(x, wet, donor, frac, rate, pos, value, var)


def spread(x, shift):
    lane = iota(x.shape, 1)
    return jnp.where(
        lane < 64, pltpu.roll(x, (127 - shift) % 128, 1), pltpu.roll(x, 63 - shift, 1)
    )


def beside(x):
    hi, lo = split(x)
    return jnp.concatenate([hi, lo], axis=1)


def doubled(both):
    left = jnp.where(iota((64, 128), 1) < 64, 1.0, 0.0)
    left, right = left.astype(BF16), (1.0 - left).astype(BF16)
    hi, lo = both[:, :128], both[:, 128:]
    hi = jnp.concatenate([hi * left, hi * right], axis=0)
    lo = jnp.concatenate([lo * left, lo * right], axis=0)
    return jnp.concatenate(
        [
            jnp.concatenate([hi, lo], axis=1),
            jnp.concatenate([hi, jnp.zeros((128, 128), BF16)], axis=1),
        ],
        axis=0,
    )


def times(both, weights):
    product = jnp.dot(both, weights, preferred_element_type=F32)
    return product[:, :128] + product[:, 128:]


def weights_kernel(
    w5, e5, attr, listed, live, fs1,
    every, f1,
    out, cols, rim, mean, picked, base, taper, force, system, drive,
    own, swap_s, swap_r, row_s, row_r, keep_s, side_s, side_r, corner_s, corner_r,
):
    t = lax.axis_index("task")
    s = lax.axis_index("patch")
    up, down = lax.rem(s + STRIPS - 1, STRIPS), lax.rem(s + 1, STRIPS)
    peer = {k: lax.rem(t + k, TASKS) for k in range(TASKS)}
    right, left = peer[1], peer[3]
    greet(
        [(peer[k], s) for k in (1, 2, 3)]
        + [(t, up), (t, down)]
        + [(x, y) for x in (right, left) for y in (up, down)]
    )
    mine = pl.ds(pl.multiple_of(16 * t, 16), 16)
    here_cols = pl.ds(pl.multiple_of(256 * t, 256), 256)
    own_copy = pltpu.make_async_copy(fs1.at[:, :, :, here_cols], f1.at[mine], own.at[0])
    own_copy.start()
    swaps = []
    for k in (1, 2, 3):
        to_cols = pl.ds(pl.multiple_of(256 * peer[k], 256), 256)
        copy = sender(
            fs1.at[:, :, :, to_cols], f1.at[mine], swap_s.at[k - 1], swap_r.at[k - 1], (peer[k], s)
        )
        copy.start()
        swaps.append(copy)

    def rows_of(n):
        part = pl.ds(n * (GROUP // 2), GROUP // 2)
        there = pl.ds(1 + n * (GROUP // 2), GROUP // 2)
        copies = []
        for a in range(2):
            copies.append(
                sender(
                    out.at[a, part], every.at[3 - 3 * a, there],
                    row_s.at[a, n], row_r.at[a, n], (t, (up, down)[a]),
                )
            )
            copies.append(
                pltpu.make_async_copy(out.at[a, part], every.at[1 + a, there], keep_s.at[a, n])
            )
        return copies

    lane = iota((8, 128), 1)
    sub = iota((8, 128), 0)

    def place(st, carry):
        for src in range(TASKS):
            tile = e5[st, src]
            for m in range(16):
                rim[16 * src + m] = pltpu.roll(tile, (128 - 8 * m) % 128, 1) if m else tile
        rows = pl.ds(pl.multiple_of(8 * st, 8), 8)
        means, rim_means = [], []
        for r in range(8):
            whole = w5[st, :, r, :]
            mu = jnp.sum(whole, axis=0, keepdims=True) * (1.0 / 64)
            dev = whole - mu
            cols[4:260, st, r, :] = jnp.concatenate([dev, dev], axis=0).T
            means.append(mu)
            whole = rim[:, r, :]
            mu = jnp.sum(whole, axis=0, keepdims=True) * (1.0 / 64)
            dev = whole - mu
            turned = jnp.concatenate([dev, dev], axis=0).T
            cols[0:4, st, r, :] = turned[0:4]
            cols[260:264, st, r, :] = turned[4:8]
            rim_means.append(mu)
        mean[rows, 0:256] = jnp.concatenate(means, axis=0)
        mean[rows, 256:384] = jnp.concatenate(rim_means, axis=0)
        return carry

    lax.fori_loop(0, 5, place, 0)

    spot = iota((384, 128), 0)
    coarse = iota((384, 128), 1)
    lane_of = iota((40, 384), 1)
    known = jnp.where(lane_of < 264, mean[...], 0.0)
    for q in range(4):
        want = jnp.where(
            coarse == 0, 256 + q, jnp.where(coarse == 65, 260 + q, 4 * coarse - 4 + q)
        )
        picked[q] = jnp.dot(
            known,
            jnp.where((spot == want) & (coarse < 66), 1.0, 0.0),
            precision=lax.Precision.HIGHEST,
            preferred_element_type=F32,
        )
    flat = listed[...]
    block_col = 4 * (iota((128, 32), 0) % 64) + 256 * t - 4
    code = ((flat // 8192 - (s - 2)) * 9 + flat % 8192 // 8 - block_col) * 8 + flat % 8
    code = code.astype(F32).T.astype(jnp.int32)
    pick = iota((64, 128), 0)
    into = iota((64, 128), 1)
    counts = live[...].astype(F32)
    alive = jnp.dot(
        counts, jnp.where(pick == into, 1.0, 0.0), preferred_element_type=F32
    )[0:1] + jnp.dot(counts, jnp.where(pick == into - 64, 1.0, 0.0), preferred_element_type=F32)[1:2]
    for slot in range(32):
        kept = jnp.where(alive > slot, code[slot : slot + 1, :], -100000)
        base[slot] = jnp.broadcast_to(kept, (8, 128)) - sub

    point_row = jnp.where(lane < 64, 1.5, 5.5)
    height = sub.astype(F32)
    taper[45] = jnp.zeros((8, 128), F32)

    def weigh(st, carry):
        for cr in range(9):
            q, shift = (cr - 4) % 4, (cr - 4) // 4
            row = spread(attr[st, 0, 8 * q : 8 * q + 8, :], shift)
            value = spread(attr[st, 1, 8 * q : 8 * q + 8, :], shift)
            var = spread(attr[st, 2, 8 * q : 8 * q + 8, :], shift)
            tile = (st * 9 + cr) * 8
            count = jnp.zeros((8, 128), F32)
            for slot in range(32):
                count = count + jnp.where(base[slot] == tile, 1.0, 0.0)
            apart = row + (8.0 * (st - 2).astype(F32)) - point_row
            dist = apart * apart + (cr - 5.5) ** 2
            weight = count * jnp.exp(dist * (-1.0 / 1152.0)) / var
            pull = weight * value
            total = jnp.zeros((8, 128), F32)
            pulled = jnp.zeros((8, 128), F32)
            for k in range(8):
                hit = row[k : k + 1] == height
                total = total + jnp.where(hit, weight[k : k + 1], 0.0)
                pulled = pulled + jnp.where(hit, pull[k : k + 1], 0.0)
            centre = spread(picked[q, pl.ds(pl.multiple_of(8 * st, 8), 8), :], shift)
            taper[cr * 5 + st] = total
            force[cr * 5 + st] = pulled - total * centre
        return carry

    lax.fori_loop(0, 5, weigh, 0)

    tall_lane = iota((368, 128), 1)
    eye = jnp.where(iota((64, 128), 0) == iota((64, 128), 1) % 64, 1.0, 0.0)

    def gram(b):
        index = jnp.where(lane < 64, b, 64 + b)
        near = cols[pl.ds(4 * b, 10)].reshape(400, 128)[:368]
        spread_taper = jnp.concatenate(
            [jnp.take_along_axis(taper[k], index, axis=1) for k in range(46)], axis=0
        )
        spread_force = jnp.concatenate(
            [jnp.take_along_axis(force[k], index, axis=1) for k in range(45)], axis=0
        )
        s_hi, s_lo = split(near * spread_taper)
        n_hi = near.astype(BF16).astype(F32)
        both = jnp.where(tall_lane < 64, n_hi, near - n_hi).astype(BF16)
        product = lax.dot_general(
            both,
            jnp.concatenate([s_hi, s_lo], axis=1),
            (((0,), (0,)), ((), ())),
            preferred_element_type=F32,
        )
        product = product[:64] + product[64:]
        return (
            product[:, :128] + product[:, 128:] + 63.0 * eye,
            jnp.sum(near[:360] * spread_force, axis=0, keepdims=True),
        )

    def keep(k, made):
        system[k] = made[0]
        drive[k] = jnp.broadcast_to(made[1], (8, 128))

    for k in range(GROUP):
        keep(k, gram(k))

    half = iota((64, 128), 1) < 64

    def solve(n, carry):
        nears, inverses, norms = [], [], []
        systems = [system[k] for k in range(GROUP)]
        drives = [drive[k][:1] for k in range(GROUP)]
        later = jnp.minimum(n + 1, 64 // GROUP - 1) * GROUP
        made = []

        def share(n):
            for k in range(n * GROUP // (2 * NS_ITERS), (n + 1) * GROUP // (2 * NS_ITERS)):
                made.append(gram(later + k))

        for x in systems:
            squares = jnp.sum(x * x, axis=0, keepdims=True)
            left = iota((1, 128), 1) < 64
            one = jnp.sum(jnp.where(left, squares, 0.0), axis=1, keepdims=True)
            two = jnp.sum(jnp.where(left, 0.0, squares), axis=1, keepdims=True)
            norm = jnp.sqrt(jnp.where(left, one, two))
            norms.append(norm)
            nears.append(x / norm)
            inverses.append(None)
        for turn in range(NS_ITERS):
            share(2 * turn)
            parts = [beside(x) for x in nears]
            weights = [doubled(x) for x in parts]
            if turn == 0:
                inverses = [1.5 * eye - 0.5 * x for x in nears]
                squared = [times(x, y) for x, y in zip(parts, weights)]
            elif turn < NS_ITERS - 1:
                squared = []
                for k in range(GROUP):
                    product = times(
                        jnp.concatenate([parts[k], beside(inverses[k])], axis=0), weights[k]
                    )
                    squared.append(product[:64])
                    inverses[k] = 1.5 * inverses[k] - 0.5 * product[64:]
            else:
                inverses = [
                    1.5 * x - 0.5 * times(beside(x), y) for x, y in zip(inverses, weights)
                ]
            share(2 * turn + 1)
            if turn < NS_ITERS - 1:
                nears = [
                    2.25 * x - 1.5 * y + 0.25 * times(beside(y), z)
                    for x, y, z in zip(nears, squared, weights)
                ]

        def standing(x):
            one = jnp.sum(jnp.where(half, x, 0.0), axis=1, keepdims=True)
            two = jnp.sum(jnp.where(half, 0.0, x), axis=1, keepdims=True)
            return jnp.where(half, one, two)

        finals = []
        for k in range(GROUP):
            z = inverses[k]
            once = jnp.sum(z * standing(eye * drives[k]), axis=0, keepdims=True)
            drift = standing(z * (once / norms[k]))
            finals.append(jnp.sqrt(63.0 / norms[k]) * z + drift)
        for k in range(0, GROUP, 2):
            g = n * (GROUP // 2) + k // 2
            out[0, g] = jnp.where(half, finals[k], pltpu.roll(finals[k + 1], 64, 1))
            out[1, g] = jnp.where(half, pltpu.roll(finals[k], 64, 1), finals[k + 1])
        for k in range(GROUP):
            keep(k, made[k])
        for copy in rows_of(n):
            copy.start()
        return carry

    lax.fori_loop(0, 64 // GROUP, solve, 0)

    sides = []
    for i, (to, at, there) in enumerate([(right, 31, 0), (left, 0, 33)]):
        for a in range(2):
            sides.append(
                sender(
                    out.at[a, at], every.at[1 + a, there],
                    side_s.at[2 * i + a], side_r.at[2 * i + a], (to, s),
                )
            )
            sides.append(
                sender(
                    out.at[a, at], every.at[3 - 3 * a, there],
                    corner_s.at[2 * i + a], corner_r.at[2 * i + a], (to, (up, down)[a]),
                )
            )
    for copy in sides:
        copy.start()

    def settle(n, carry):
        for copy in rows_of(n):
            copy.wait()
        return carry

    lax.fori_loop(0, 64 // GROUP, settle, 0)
    for copy in sides + swaps:
        copy.wait()
    own_copy.wait()


def point_weights(w5, e5, attr5, listed, live, fs1):
    dma = pltpu.SemaphoreType.DMA
    vmem = pl.BlockSpec(memory_space=pltpu.VMEM)
    anywhere = pl.BlockSpec(memory_space=pl.ANY)
    turns = 64 // GROUP
    return pl.pallas_call(
        weights_kernel,
        out_shape=[
            jax.ShapeDtypeStruct((4, 34, 64, 128), F32),
            jax.ShapeDtypeStruct((64, 3, 8, 256), F32),
        ],
        in_specs=[vmem] * 5 + [anywhere],
        out_specs=[anywhere] * 2,
        scratch_shapes=[
            pltpu.VMEM((2, 32, 64, 128), F32),
            pltpu.VMEM((264, 5, 8, 128), F32),
            pltpu.VMEM((64, 8, 128), F32),
            pltpu.VMEM((40, 384), F32),
            pltpu.VMEM((4, 40, 128), F32),
            pltpu.VMEM((32, 8, 128), jnp.int32),
            pltpu.VMEM((46, 8, 128), F32),
            pltpu.VMEM((45, 8, 128), F32),
            pltpu.VMEM((GROUP, 64, 128), F32),
            pltpu.VMEM((GROUP, 8, 128), F32),
            dma((1,)), dma((3,)), dma((3,)), dma((2, turns)), dma((2, turns)), dma((2, turns)),
            dma((4,)), dma((4,)), dma((4,)), dma((4,)),
        ],
        compiler_params=pltpu.CompilerParams(
            collective_id=2, has_side_effects=True, vmem_limit_bytes=LIMIT
        ),
    )(w5, e5, attr5, listed, live, fs1)


def hat(x):
    return jnp.maximum(1.0 - jnp.abs(x - 1.5) * 0.25, 0.0)


def analysis_kernel(
    every_in, w5, f1, wet,
    out,
    every, f0, turned, mid, top, low, total, result,
    own, back_s, back_r,
):
    t = lax.axis_index("task")
    s = lax.axis_index("patch")
    peer = {k: lax.rem(t + k, TASKS) for k in range(TASKS)}
    load = pltpu.make_async_copy(w5.at[2], f0, own.at[0])
    load.start()
    fetch = pltpu.make_async_copy(every_in, every, own.at[1])
    fetch.start()
    greet([(peer[k], s) for k in (1, 2, 3)])

    total[...] = jnp.zeros_like(total)
    load.wait()
    cols = pl.ds(pl.multiple_of(256 * t, 256), 256)

    def field(lev, r):
        return f0[:, r, :] if lev == 0 else f1[:, lev - 1, r, :]

    for lev in range(4):
        for r in range(8):
            whole = field(lev, r)
            dev = whole - jnp.sum(whole, axis=0, keepdims=True) * (1.0 / 64)
            turned[10:266, r // 2, 4 * (r % 2) + lev, :] = jnp.concatenate([dev, dev], axis=0).T

    lane = iota((8, 128), 1)
    row = iota((8, 128), 0) // 4
    second = jnp.where(lane < 64, 0.0, 4.0)
    first_strip = jnp.where(s == 0, 1.0, 0.0)
    last_strip = jnp.where(s == STRIPS - 1, 1.0, 0.0)

    def row_share(a, k):
        r = (2 * k + row).astype(F32)
        if a == -1:
            return hat(r + 4.0) * (1.0 - first_strip)
        if a == 0:
            return hat(r) + hat(r + 4.0) * first_strip
        if a == 1:
            return hat(r - 4.0) + hat(r - 8.0) * last_strip
        return hat(r - 8.0) * (1.0 - last_strip)

    left = iota((8, 8, 128), 2) < 64

    def parted(x, share):
        x = x * share[None]
        high = x.astype(BF16).astype(F32)
        return jnp.where(left, high, x - high)

    for ref in (mid, top, low):
        ref[...] = jnp.zeros_like(ref)

    def part(n, carry):
        for k, a, ref in ((0, -1, top), (3, 1, low)):
            x = turned[pl.ds(8 * n + 10, 8), k]
            both = jnp.concatenate(
                [parted(x, row_share(a, k)), parted(x, row_share(a + 1, k))], axis=2
            )
            ref[pl.ds(pl.multiple_of(64 * n + 80, 16), 64)] = both.reshape(64, 256).astype(BF16)
        pieces = []
        for k in (1, 2):
            x = turned[pl.ds(8 * n + 10, 8), k]
            pieces.append(
                jnp.concatenate([parted(x, row_share(0, k)), parted(x, row_share(1, k))], axis=2)
            )
        both = jnp.stack(pieces, axis=1)
        mid[pl.ds(pl.multiple_of(128 * n + 160, 16), 128)] = both.reshape(128, 256).astype(BF16)
        return carry

    lax.fori_loop(0, 32, part, 0)

    def col_share(g):
        first = jnp.where((g == 0) & (t == 0), 1.0, 0.0)
        last = jnp.where((g == 31) & (t == TASKS - 1), 1.0, 0.0)
        alive = jnp.where(
            ((g == -1) & (t == 0)) | ((g == 32) & (t == TASKS - 1)), 0.0, 1.0
        )
        shares = []
        for c in range(12):
            x = (c - 2.0) - second
            share = hat(x)
            if c in (2, 3):
                share = share + jnp.where(lane < 64, hat(x + 4.0), 0.0) * first
            if c in (8, 9):
                share = share + jnp.where(lane < 64, 0.0, hat(x - 4.0)) * last
            shares.append(share * alive)
        return shares

    def paired(x):
        hi, lo = split(x)
        zero = jnp.zeros((64, 128), BF16)
        return jnp.concatenate(
            [jnp.concatenate([hi, lo], axis=1), jnp.concatenate([hi, zero], axis=1)], axis=0
        )

    def blend(n, carry):
        g = n - 1
        shares = col_share(g)
        operands = [paired(every[a, n]) for a in range(4)]
        for a, ref, height, first in ((0, top, 8, 0), (1, mid, 16, 1), (2, low, 8, 3)):
            rows = ref[pl.ds(pl.multiple_of(height * (8 * g + 8), 16), 12 * height)]
            product = jnp.dot(
                rows,
                jnp.concatenate([operands[a], operands[a + 1]], axis=0),
                preferred_element_type=F32,
            )
            product = (product[:, :128] + product[:, 128:]).reshape(12, height // 8, 8, 128)
            for c in range(12):
                total[8 * g + 8 + c, first : first + height // 8] += product[c] * shares[c][None]
        return carry

    fetch.wait()
    mine = pl.ds(pl.multiple_of(16 * t, 16), 16)
    copies = []
    for h in range(2):
        if h == 0:
            lax.fori_loop(0, 18, blend, 0)
        else:
            lax.fori_loop(18, 34, blend, 0)
        here = slice(128 * h, 128 * h + 128)
        ocean_cols = pl.ds(pl.multiple_of(256 * t + 128 * h, 128), 128)
        for r in range(8):
            ocean = wet[r : r + 1, ocean_cols].astype(F32)
            for lev in range(4):
                back = total[10 + 128 * h : 138 + 128 * h, r // 2, 4 * (r % 2) + lev, :].T
                whole = field(lev, r)[:, here]
                dev = whole - jnp.sum(whole, axis=0, keepdims=True) * (1.0 / 64)
                result[:, lev, r, here] = whole + ocean * (back[:64] + back[64:] - dev)
        copy = pltpu.make_async_copy(
            result.at[mine, :, :, here], out.at[:, :, :, ocean_cols], own.at[2 + h]
        )
        copy.start()
        copies.append(copy)
        for k in (1, 2, 3):
            theirs = pl.ds(pl.multiple_of(16 * peer[k], 16), 16)
            copy = sender(
                result.at[theirs, :, :, here], out.at[:, :, :, ocean_cols],
                back_s.at[3 * h + k - 1], back_r.at[3 * h + k - 1], (peer[k], s),
            )
            copy.start()
            copies.append(copy)
    for copy in copies:
        copy.wait()


def analysed(every, w5, f1, wet):
    dma = pltpu.SemaphoreType.DMA
    vmem = pl.BlockSpec(memory_space=pltpu.VMEM)
    anywhere = pl.BlockSpec(memory_space=pl.ANY)
    return pl.pallas_call(
        analysis_kernel,
        out_shape=jax.ShapeDtypeStruct((16, 4, 8, 1024), F32),
        in_specs=[anywhere, anywhere, vmem, vmem],
        out_specs=anywhere,
        scratch_shapes=[
            pltpu.VMEM((4, 34, 64, 128), F32),
            pltpu.VMEM((64, 8, 256), F32),
            pltpu.VMEM((SPAN, 4, 8, 128), F32),
            pltpu.VMEM((SPAN * 16, 256), BF16),
            pltpu.VMEM((SPAN * 8, 256), BF16),
            pltpu.VMEM((SPAN * 8, 256), BF16),
            pltpu.VMEM((SPAN, 4, 8, 128), F32),
            pltpu.VMEM((64, 4, 8, 256), F32),
            dma((4,)), dma((6,)), dma((6,)),
        ],
        compiler_params=pltpu.CompilerParams(
            collective_id=1, has_side_effects=True, vmem_limit_bytes=LIMIT
        ),
    )(every, w5, f1, wet)


def body(
    trials_initial_dye,
    diffusivity,
    wet_mask,
    deeper_donor_tier,
    shallower_tier_fraction,
    obs_pos,
    obs_value,
    obs_var,
    observation_list,
    obs_count,
):
    w5, fs1, e5, attr5 = forecast(
        trials_initial_dye,
        wet_mask,
        deeper_donor_tier,
        shallower_tier_fraction,
        diffusivity,
        obs_pos.reshape(64, 128),
        obs_value.reshape(64, 128),
        obs_var.reshape(64, 128),
    )
    every, f1 = point_weights(
        w5, e5, attr5, observation_list.reshape(128, 32), obs_count, fs1
    )
    return analysed(every, w5, f1, wet_mask)


def solution(mesh):
    return jax.shard_map(
        body,
        mesh=mesh,
        in_specs=(
            P("task", None, "patch", None),
            P(),
            P("patch", None),
            P(None, "patch", None),
            P(None, "patch", None),
            P("patch"),
            P("patch"),
            P("patch"),
            P("patch", "task", None),
            P("patch", "task"),
        ),
        out_specs=P("task", None, "patch", None),
        check_vma=False,
    )
```

```python
import functools

import jax
import jax.numpy as jnp
from jax import lax
from jax.experimental import pallas as pl
from jax.experimental.pallas import tpu as pltpu
from jax.sharding import PartitionSpec as P

MESH = pl.DeviceIdType.MESH
F32 = jnp.float32
BF16 = jnp.bfloat16
STEPS = 4
NS_ITERS = 6
TASKS = 4
STRIPS = 32
GROUP = 8
SPAN = 276
SOLVES = 64 // GROUP
LIMIT = 60 * 1024 * 1024


def iota(shape, dim):
    return lax.broadcasted_iota(jnp.int32, shape, dim)


def split(x):
    hi = x.astype(BF16)
    return hi, (x - hi.astype(F32)).astype(BF16)


def greet(peers):
    barrier = pltpu.get_barrier_semaphore()
    for peer in peers:
        pl.semaphore_signal(barrier, inc=1, device_id=peer, device_id_type=MESH)
    pl.semaphore_wait(barrier, len(peers))


def sender(src, dst, ss, rs, to):
    return pltpu.make_async_remote_copy(
        src_ref=src, dst_ref=dst, send_sem=ss, recv_sem=rs, device_id=to, device_id_type=MESH
    )


def spread(x, shift):
    lane = iota(x.shape, 1)
    return jnp.where(
        lane < 64, pltpu.roll(x, (127 - shift) % 128, 1), pltpu.roll(x, 63 - shift, 1)
    )


def beside(x):
    hi, lo = split(x)
    return jnp.concatenate([hi, lo], axis=1)


def doubled(both):
    left = jnp.where(iota((64, 128), 1) < 64, 1.0, 0.0)
    left, right = left.astype(BF16), (1.0 - left).astype(BF16)
    hi, lo = both[:, :128], both[:, 128:]
    hi = jnp.concatenate([hi * left, hi * right], axis=0)
    lo = jnp.concatenate([lo * left, lo * right], axis=0)
    return jnp.concatenate(
        [
            jnp.concatenate([hi, lo], axis=1),
            jnp.concatenate([hi, jnp.zeros((128, 128), BF16)], axis=1),
        ],
        axis=0,
    )


def times(both, weights):
    product = jnp.dot(both, weights, preferred_element_type=F32)
    return product[:, :128] + product[:, 128:]


def hat(x):
    return jnp.maximum(1.0 - jnp.abs(x - 1.5) * 0.25, 0.0)


def kernel(
    x, wet, donor, frac, rate, pos, value, var, listed, live,
    out,
    hal, whal, mixing, fs0, fs1, es, attr,
    w5, e5, attr5, f1,
    every, cols, rim, mean, picked, base, taper, force, system, drive,
    turned, mid, top, low, total, result,
    halo_s, halo_r, wet_s, wet_r, attr_s, attr_r, own, swap_s, swap_r, rim_s, rim_r,
    win_s, win_r, edge_s, edge_r,
    deep_s, deep_r, row_s, row_r, side_s, side_r, corner_s, corner_r, back_s, back_r,
):
    t = lax.axis_index("task")
    s = lax.axis_index("patch")
    strip = {d: lax.rem(s + d + STRIPS, STRIPS) for d in (-2, -1, 1, 2)}
    up, down = strip[-1], strip[1]
    peer = {k: lax.rem(t + k, TASKS) for k in range(TASKS)}
    beyond = ((peer[1], 31, 0), (peer[3], 0, 33))
    way = 1 - 2 * lax.rem(s, 2)
    mate = s + way
    second = lax.rem(s + 2 * way + STRIPS, STRIPS)
    other = lax.rem(s - way + STRIPS, STRIPS)
    greet(
        [(t, strip[d]) for d in (-2, -1, 1, 2)]
        + [(peer[k], s) for k in (1, 2, 3)]
        + [(peer[k], y) for k in (1, 3) for y in (up, down)]
    )

    def send(src, dst, ss, rs, to):
        copy = sender(src, dst, ss, rs, to)
        copy.start()
        return copy

    wet_copies = []
    halo_copies = []
    for i, d in enumerate((-1, 1)):
        part = pl.ds(4 * i, 4)
        wet_copies.append(
            send(wet.at[part], whal.at[part], wet_s.at[i], wet_r.at[i], (t, strip[d]))
        )
    for c in range(4):
        members = pl.ds(4 * c, 4)
        for i, d in enumerate((-1, 1)):
            part = pl.ds(4 * i, 4)
            halo_copies.append(
                send(
                    x.at[members, :, part],
                    hal.at[members, :, part],
                    halo_s.at[2 * c + i],
                    halo_r.at[2 * c + i],
                    (t, strip[d]),
                )
            )

    facts = jnp.concatenate(
        [(pos[...] // 1024).astype(F32).T, value[...].T, var[...].T], axis=0
    )
    spot = iota((64, 128), 0)
    coarse = iota((64, 128), 1) - 1
    gathered = jnp.zeros((96, 128), F32)
    for m in range(4):
        taken = (spot == (coarse + 4) // 4 - 1 + 16 * t) & ((coarse + 4) % 4 == m)
        rows = jnp.concatenate([facts[128 * i + 32 * m : 128 * i + 32 * m + 32] for i in range(3)])
        gathered = gathered + jnp.dot(
            rows,
            jnp.where(taken, 1.0, 0.0),
            precision=lax.Precision.HIGHEST,
            preferred_element_type=F32,
        )
    lane96 = iota((32, 128), 1)
    known = (lane96 - 1 + 64 * t >= 0) & (lane96 - 1 + 64 * t < 256)
    attr[0] = gathered[0:32]
    attr[1] = gathered[32:64]
    attr[2] = jnp.where(known, gathered[64:96], 1.0)
    attr_copies = [
        send(attr, attr5.at[2 - d], attr_s.at[i], attr_r.at[i], (t, strip[d]))
        for i, d in enumerate((-2, -1, 1, 2))
    ]
    own_attr = pltpu.make_async_copy(attr, attr5.at[2], own.at[0])
    own_attr.start()

    sub = iota((8, 128), 0)
    lane = iota((8, 128), 1)
    below = jnp.where(s < STRIPS - 1, 1.0, 0.0)
    above = jnp.where(s > 0, 1.0, 0.0)
    inside = jnp.where(sub < 4, below, above)
    for copy in wet_copies:
        copy.wait()
    ocean = wet[...].astype(F32)
    ocean_halo = whal[...].astype(F32) * jnp.where(iota((8, 1024), 0) < 4, below, above)
    for lev in range(4):
        for i, mask in enumerate((ocean, ocean_halo)):
            mixing[lev, i, 0] = mask * (1.0 - 4.0 * rate[lev])
            mixing[lev, i, 1] = mask * rate[lev]
    es[...] = jnp.zeros_like(es)

    def advance(x, y, lev, which):
        fresh = []
        east = [pltpu.roll(a, 127, 1) for a in x] + [jnp.zeros((8, 128), F32)]
        west = [jnp.zeros((8, 128), F32)] + [pltpu.roll(a, 1, 1) for a in x]
        for j in range(8):
            around = (
                jnp.where(sub == 7, pltpu.roll(y[j], 7, 0), pltpu.roll(x[j], 7, 0))
                + jnp.where(sub == 0, pltpu.roll(y[j], 1, 0), pltpu.roll(x[j], 1, 0))
                + jnp.where(lane == 127, east[j + 1], east[j])
                + jnp.where(lane == 0, west[j], west[j + 1])
            )
            here = slice(128 * j, 128 * j + 128)
            fresh.append(
                mixing[lev, which, 0, :, here] * x[j] + mixing[lev, which, 1, :, here] * around
            )
        return fresh

    def member(m, carry):
        levels = []
        for lev in range(4):
            here = [x[m, lev, :, 128 * j : 128 * j + 128] for j in range(8)]
            rest = [hal[m, lev, :, 128 * j : 128 * j + 128] * inside for j in range(8)]
            for step in range(STEPS):
                fresh = advance(here, rest, lev, 0)
                if step < STEPS - 1:
                    rest = advance(rest, here, lev, 1)
                here = fresh
            levels.append(here)
        surface = []
        for j in range(8):
            here = slice(128 * j, 128 * j + 128)
            for lev in range(4):
                tier = donor[lev, :, here]
                first, second = tier == 0, tier == 1
                one, two, three, four = (levels[i][j] for i in range(4))
                near = jnp.where(first, one, jnp.where(second, two, three))
                far = jnp.where(first, two, jnp.where(second, three, four))
                share = frac[lev, :, here]
                mixed = (1.0 - share) * near + share * far
                if lev:
                    fs1[m, lev - 1, :, here] = mixed
                else:
                    fs0[m, :, here] = mixed
                    surface.append(mixed)
        for k in range(TASKS):
            edge = jnp.where(lane >= 124, surface[(2 * k - 1) % 8], surface[(2 * k + 2) % 8])
            es[k] = jnp.where(lane // 8 == m, pltpu.roll(edge, m * 8 + 4, 1), es[k])
        return carry

    here_cols = pl.ds(pl.multiple_of(256 * t, 256), 256)
    local = []
    swaps = {}
    windows = {}

    def block(src, c):
        return pl.ds(pl.multiple_of(16 * src + 4 * c, 4), 4)

    def exchange(c):
        chunk = pl.ds(4 * c, 4)
        copy = pltpu.make_async_copy(
            fs0.at[chunk, :, here_cols], w5.at[2, block(t, c)], own.at[1 + c]
        )
        copy.start()
        local.append(copy)
        for k in (1, 2, 3):
            to = peer[k]
            cols = pl.ds(pl.multiple_of(256 * to, 256), 256)
            i = 3 * c + k - 1
            swaps[c, k] = send(
                fs0.at[chunk, :, cols], w5.at[2, block(t, c)], swap_s.at[i], swap_r.at[i], (to, s)
            )

    def forward(c):
        for k in range(TASKS):
            src = lax.rem(t - k + TASKS, TASKS)
            part = block(src, c)
            if k:
                swaps[c, k].wait_recv()
                held = w5.at[2, part]
            else:
                held = fs0.at[pl.ds(4 * c, 4), :, here_cols]
            for j, (to, slot) in enumerate(
                ((other, 2 + way), (second, 2 - 2 * way), (mate, 2 - way))
            ):
                i = 16 * j + 4 * c + k
                windows[j, c, k] = send(
                    held, w5.at[slot, part], win_s.at[i], win_r.at[i], (t, to)
                )

    def relay(c):
        for k in range(TASKS):
            src = lax.rem(t - k + TASKS, TASKS)
            part = block(src, c)
            windows[0, c, k].wait_recv()
            i = 48 + 4 * c + k
            windows[3, c, k] = send(
                w5.at[2 - way, part], w5.at[2 - 2 * way, part],
                win_s.at[i], win_r.at[i], (t, mate),
            )

    for c in range(4):
        halo_copies[2 * c].wait_recv()
        halo_copies[2 * c + 1].wait_recv()
        lax.fori_loop(4 * c, 4 * c + 4, member, 0)
        exchange(c)
        if c == 3:
            rims = []
            for k in (1, 2, 3):
                rims.append(
                    send(
                        es.at[peer[k]], e5.at[2, t], rim_s.at[k - 1], rim_r.at[k - 1], (peer[k], s)
                    )
                )
            own_rim = pltpu.make_async_copy(es.at[t], e5.at[2, t], own.at[5])
            own_rim.start()
        if c:
            forward(c - 1)
    forward(3)
    own_rim.wait()
    for copy in rims:
        copy.wait_recv()
    edges = [
        send(e5.at[2], e5.at[2 - d], edge_s.at[i], edge_r.at[i], (t, strip[d]))
        for i, d in enumerate((-2, -1, 1, 2))
    ]
    mine = pl.ds(pl.multiple_of(16 * t, 16), 16)
    own_deep = pltpu.make_async_copy(fs1.at[:, :, :, here_cols], f1.at[mine], own.at[6])
    own_deep.start()
    deeps = []
    for k in (1, 2, 3):
        to_cols = pl.ds(pl.multiple_of(256 * peer[k], 256), 256)
        deeps.append(
            send(
                fs1.at[:, :, :, to_cols], f1.at[mine],
                deep_s.at[k - 1], deep_r.at[k - 1], (peer[k], s),
            )
        )

    def place(st):
        for src in range(TASKS):
            tile = e5[st, src]
            for m in range(16):
                rim[16 * src + m] = pltpu.roll(tile, (128 - 8 * m) % 128, 1) if m else tile
        rows = pl.ds(pl.multiple_of(8 * st, 8), 8)
        means, rim_means = [], []
        for r in range(8):
            whole = w5[st, :, r, :]
            mu = jnp.sum(whole, axis=0, keepdims=True) * (1.0 / 64)
            dev = whole - mu
            cols[4:260, st, r, :] = jnp.concatenate([dev, dev], axis=0).T
            means.append(mu)
            whole = rim[:, r, :]
            mu = jnp.sum(whole, axis=0, keepdims=True) * (1.0 / 64)
            dev = whole - mu
            turned = jnp.concatenate([dev, dev], axis=0).T
            cols[0:4, st, r, :] = turned[0:4]
            cols[260:264, st, r, :] = turned[4:8]
            rim_means.append(mu)
        mean[rows, 0:256] = jnp.concatenate(means, axis=0)
        mean[rows, 256:384] = jnp.concatenate(rim_means, axis=0)

    for copy in local:
        copy.wait()
    place(2)
    flat = listed[...]
    block_col = 4 * (iota((128, 32), 0) % 64) + 256 * t - 4
    code = ((flat // 8192 - (s - 2)) * 9 + flat % 8192 // 8 - block_col) * 8 + flat % 8
    code = code.astype(F32).T.astype(jnp.int32)
    pick = iota((64, 128), 0)
    into = iota((64, 128), 1)
    counts = live[...].astype(F32)
    alive = jnp.dot(
        counts, jnp.where(pick == into, 1.0, 0.0), preferred_element_type=F32
    )[0:1] + jnp.dot(counts, jnp.where(pick == into - 64, 1.0, 0.0), preferred_element_type=F32)[1:2]
    for slot in range(32):
        kept = jnp.where(alive > slot, code[slot : slot + 1, :], -100000)
        base[slot] = jnp.broadcast_to(kept, (8, 128)) - sub

    for copy in attr_copies:
        copy.wait()
    own_attr.wait()
    point_row = jnp.where(lane < 64, 1.5, 5.5)
    height = sub.astype(F32)
    taper[45] = jnp.zeros((8, 128), F32)

    def weigh(st, carry):
        for cr in range(9):
            q, shift = (cr - 4) % 4, (cr - 4) // 4
            row = spread(attr5[st, 0, 8 * q : 8 * q + 8, :], shift)
            value = spread(attr5[st, 1, 8 * q : 8 * q + 8, :], shift)
            var = spread(attr5[st, 2, 8 * q : 8 * q + 8, :], shift)
            tile = (st * 9 + cr) * 8
            count = jnp.zeros((8, 128), F32)
            for slot in range(32):
                count = count + jnp.where(base[slot] == tile, 1.0, 0.0)
            apart = row + (8.0 * (st - 2).astype(F32)) - point_row
            dist = apart * apart + (cr - 5.5) ** 2
            weight = count * jnp.exp(dist * (-1.0 / 1152.0)) / var
            pull = weight * value
            held = jnp.zeros((8, 128), F32)
            pulled = jnp.zeros((8, 128), F32)
            for k in range(8):
                hit = row[k : k + 1] == height
                held = held + jnp.where(hit, weight[k : k + 1], 0.0)
                pulled = pulled + jnp.where(hit, pull[k : k + 1], 0.0)
            taper[cr * 5 + st] = held
            force[cr * 5 + st] = pulled
        return carry

    lax.fori_loop(0, 5, weigh, 0)

    def field(lev, r):
        return w5[2, :, r, :] if lev == 0 else f1[:, lev - 1, r, :]

    def turn(lev):
        for r in range(8):
            whole = field(lev, r)
            dev = whole - jnp.sum(whole, axis=0, keepdims=True) * (1.0 / 64)
            turned[10:266, r // 2, 4 * (r % 2) + lev, :] = jnp.concatenate([dev, dev], axis=0).T

    total[...] = jnp.zeros_like(total)
    for ref in (mid, top, low):
        ref[...] = jnp.zeros_like(ref)
    turn(0)

    for c in range(4):
        relay(c)
    for copy in edges:
        copy.wait()
    for j, slot in ((2, 2 + way), (0, 2 - way), (1, 2 - 2 * way), (3, 2 + 2 * way)):
        if j:
            for c in range(4):
                for k in range(TASKS):
                    windows[j, c, k].wait_recv()
        place(slot)

    spot = iota((384, 128), 0)
    coarse = iota((384, 128), 1)
    lane_of = iota((40, 384), 1)
    known = jnp.where(lane_of < 264, mean[...], 0.0)
    for q in range(4):
        want = jnp.where(
            coarse == 0, 256 + q, jnp.where(coarse == 65, 260 + q, 4 * coarse - 4 + q)
        )
        picked[q] = jnp.dot(
            known,
            jnp.where((spot == want) & (coarse < 66), 1.0, 0.0),
            precision=lax.Precision.HIGHEST,
            preferred_element_type=F32,
        )
    def recentre(st, carry):
        for cr in range(9):
            q, shift = (cr - 4) % 4, (cr - 4) // 4
            centre = spread(picked[q, pl.ds(pl.multiple_of(8 * st, 8), 8), :], shift)
            force[cr * 5 + st] = force[cr * 5 + st] - taper[cr * 5 + st] * centre
        return carry

    lax.fori_loop(0, 5, recentre, 0)

    tall_lane = iota((368, 128), 1)
    eye = jnp.where(iota((64, 128), 0) == iota((64, 128), 1) % 64, 1.0, 0.0)

    def gram(b):
        index = jnp.where(lane < 64, b, 64 + b)
        near = cols[pl.ds(4 * b, 10)].reshape(400, 128)[:368]
        spread_taper = jnp.concatenate(
            [jnp.take_along_axis(taper[k], index, axis=1) for k in range(46)], axis=0
        )
        spread_force = jnp.concatenate(
            [jnp.take_along_axis(force[k], index, axis=1) for k in range(45)], axis=0
        )
        s_hi, s_lo = split(near * spread_taper)
        n_hi = near.astype(BF16).astype(F32)
        both = jnp.where(tall_lane < 64, n_hi, near - n_hi).astype(BF16)
        product = lax.dot_general(
            both,
            jnp.concatenate([s_hi, s_lo], axis=1),
            (((0,), (0,)), ((), ())),
            preferred_element_type=F32,
        )
        product = product[:64] + product[64:]
        return (
            product[:, :128] + product[:, 128:] + 63.0 * eye,
            jnp.sum(near[:360] * spread_force, axis=0, keepdims=True),
        )

    def keep(k, made):
        system[k] = made[0]
        drive[k] = jnp.broadcast_to(made[1], (8, 128))

    for k in range(GROUP):
        keep(k, gram(64 - GROUP + k))

    half = iota((64, 128), 1) < 64

    def rows_of(i):
        n = lax.rem(i + SOLVES - 1, SOLVES)
        part = pl.ds(1 + n * (GROUP // 2), GROUP // 2)
        return [
            sender(
                every.at[1 + a, part], every.at[3 - 3 * a, part],
                row_s.at[a, i], row_r.at[a, i], (t, (up, down)[a]),
            )
            for a in range(2)
        ]

    def sides_of():
        copies = []
        for i, (to, at, there) in enumerate(beyond):
            for a in range(2):
                copies.append(
                    sender(
                        every.at[1 + a, at + 1], every.at[1 + a, there],
                        side_s.at[2 * i + a], side_r.at[2 * i + a], (to, s),
                    )
                )
                copies.append(
                    sender(
                        every.at[1 + a, at + 1], every.at[3 - 3 * a, there],
                        corner_s.at[2 * i + a], corner_r.at[2 * i + a], (to, (up, down)[a]),
                    )
                )
        return copies

    def solve(i, carry):
        n = lax.rem(i + SOLVES - 1, SOLVES)
        nears, inverses, norms = [], [], []
        systems = [system[k] for k in range(GROUP)]
        drives = [drive[k][:1] for k in range(GROUP)]
        later = jnp.minimum(i, SOLVES - 2) * GROUP
        made = []

        def share(n):
            for k in range(n * GROUP // (2 * NS_ITERS), (n + 1) * GROUP // (2 * NS_ITERS)):
                made.append(gram(later + k))

        for x in systems:
            squares = jnp.sum(x * x, axis=0, keepdims=True)
            left = iota((1, 128), 1) < 64
            one = jnp.sum(jnp.where(left, squares, 0.0), axis=1, keepdims=True)
            two = jnp.sum(jnp.where(left, 0.0, squares), axis=1, keepdims=True)
            norm = jnp.sqrt(jnp.where(left, one, two))
            norms.append(norm)
            nears.append(x / norm)
            inverses.append(None)
        for turn in range(NS_ITERS):
            share(2 * turn)
            parts = [beside(x) for x in nears]
            weights = [doubled(x) for x in parts]
            if turn == 0:
                inverses = [1.5 * eye - 0.5 * x for x in nears]
                squared = [times(x, y) for x, y in zip(parts, weights)]
            elif turn < NS_ITERS - 1:
                squared = []
                for k in range(GROUP):
                    product = times(
                        jnp.concatenate([parts[k], beside(inverses[k])], axis=0), weights[k]
                    )
                    squared.append(product[:64])
                    inverses[k] = 1.5 * inverses[k] - 0.5 * product[64:]
            else:
                inverses = [
                    1.5 * x - 0.5 * times(beside(x), y) for x, y in zip(inverses, weights)
                ]
            share(2 * turn + 1)
            if turn < NS_ITERS - 1:
                nears = [
                    2.25 * x - 1.5 * y + 0.25 * times(beside(y), z)
                    for x, y, z in zip(nears, squared, weights)
                ]

        def standing(x):
            one = jnp.sum(jnp.where(half, x, 0.0), axis=1, keepdims=True)
            two = jnp.sum(jnp.where(half, 0.0, x), axis=1, keepdims=True)
            return jnp.where(half, one, two)

        finals = []
        for k in range(GROUP):
            z = inverses[k]
            once = jnp.sum(z * standing(eye * drives[k]), axis=0, keepdims=True)
            drift = standing(z * (once / norms[k]))
            finals.append(jnp.sqrt(63.0 / norms[k]) * z + drift)
        for k in range(0, GROUP, 2):
            g = n * (GROUP // 2) + k // 2
            every[1, g + 1] = jnp.where(half, finals[k], pltpu.roll(finals[k + 1], 64, 1))
            every[2, g + 1] = jnp.where(half, pltpu.roll(finals[k], 64, 1), finals[k + 1])
        for k in range(GROUP):
            keep(k, made[k])
        for copy in rows_of(i):
            copy.start()

        @pl.when(i == 1)
        def _():
            for copy in sides_of():
                copy.start()

        return carry

    row = iota((8, 128), 0) // 4
    offset = jnp.where(lane < 64, 0.0, 4.0)
    first_strip = jnp.where(s == 0, 1.0, 0.0)
    last_strip = jnp.where(s == STRIPS - 1, 1.0, 0.0)

    def row_share(a, k):
        r = (2 * k + row).astype(F32)
        if a == -1:
            return hat(r + 4.0) * (1.0 - first_strip)
        if a == 0:
            return hat(r) + hat(r + 4.0) * first_strip
        if a == 1:
            return hat(r - 4.0) + hat(r - 8.0) * last_strip
        return hat(r - 8.0) * (1.0 - last_strip)

    left = iota((8, 8, 128), 2) < 64

    def parted(x, share):
        x = x * share[None]
        high = x.astype(BF16).astype(F32)
        return jnp.where(left, high, x - high)

    def part(n, carry):
        for k, a, ref in ((0, -1, top), (3, 1, low)):
            x = turned[pl.ds(8 * n + 10, 8), k]
            both = jnp.concatenate(
                [parted(x, row_share(a, k)), parted(x, row_share(a + 1, k))], axis=2
            )
            ref[pl.ds(pl.multiple_of(64 * n + 80, 16), 64)] = both.reshape(64, 256).astype(BF16)
        pieces = []
        for k in (1, 2):
            x = turned[pl.ds(8 * n + 10, 8), k]
            pieces.append(
                jnp.concatenate([parted(x, row_share(0, k)), parted(x, row_share(1, k))], axis=2)
            )
        both = jnp.stack(pieces, axis=1)
        mid[pl.ds(pl.multiple_of(128 * n + 160, 16), 128)] = both.reshape(128, 256).astype(BF16)
        return carry

    def col_share(g):
        first = jnp.where((g == 0) & (t == 0), 1.0, 0.0)
        last = jnp.where((g == 31) & (t == TASKS - 1), 1.0, 0.0)
        alive = jnp.where(
            ((g == -1) & (t == 0)) | ((g == 32) & (t == TASKS - 1)), 0.0, 1.0
        )
        shares = []
        for c in range(12):
            x = (c - 2.0) - offset
            share = hat(x)
            if c in (2, 3):
                share = share + jnp.where(lane < 64, hat(x + 4.0), 0.0) * first
            if c in (8, 9):
                share = share + jnp.where(lane < 64, 0.0, hat(x - 4.0)) * last
            shares.append(share * alive)
        return shares

    def paired(x):
        hi, lo = split(x)
        zero = jnp.zeros((64, 128), BF16)
        return jnp.concatenate(
            [jnp.concatenate([hi, lo], axis=1), jnp.concatenate([hi, zero], axis=1)], axis=0
        )

    def blend(n, carry):
        g = n - 1
        shares = col_share(g)
        operands = [paired(every[a, n]) for a in range(4)]
        for a, ref, height, first in ((0, top, 8, 0), (1, mid, 16, 1), (2, low, 8, 3)):
            rows = ref[pl.ds(pl.multiple_of(height * (8 * g + 8), 16), 12 * height)]
            product = jnp.dot(
                rows,
                jnp.concatenate([operands[a], operands[a + 1]], axis=0),
                preferred_element_type=F32,
            )
            product = (product[:, :128] + product[:, 128:]).reshape(12, height // 8, 8, 128)
            for c in range(12):
                total[8 * g + 8 + c, first : first + height // 8] += product[c] * shares[c][None]
        return carry

    def finish(h):
        copies = []
        here = slice(128 * h, 128 * h + 128)
        ocean_cols = pl.ds(pl.multiple_of(256 * t + 128 * h, 128), 128)
        for r in range(8):
            ocean = wet[r : r + 1, ocean_cols].astype(F32)
            for lev in range(4):
                back = total[10 + 128 * h : 138 + 128 * h, r // 2, 4 * (r % 2) + lev, :].T
                whole = field(lev, r)[:, here]
                dev = whole - jnp.sum(whole, axis=0, keepdims=True) * (1.0 / 64)
                result[:, lev, r, here] = whole + ocean * (back[:64] + back[64:] - dev)
        copy = pltpu.make_async_copy(
            result.at[mine, :, :, here], out.at[:, :, :, ocean_cols], own.at[7 + h]
        )
        copy.start()
        copies.append(copy)
        for k in (1, 2, 3):
            theirs = pl.ds(pl.multiple_of(16 * peer[k], 16), 16)
            copies.append(
                send(
                    result.at[theirs, :, :, here], out.at[:, :, :, ocean_cols],
                    back_s.at[3 * h + k - 1], back_r.at[3 * h + k - 1], (peer[k], s),
                )
            )
        return copies

    lax.fori_loop(0, SOLVES - 1, solve, 0)

    own_deep.wait()
    for copy in deeps:
        copy.wait_recv()
    for lev in (1, 2, 3):
        turn(lev)
    lax.fori_loop(0, 32, part, 0)

    def arrived(i, carry):
        for copy in rows_of(i):
            copy.wait_recv()
        return carry

    sides = sides_of()
    lax.fori_loop(0, SOLVES - 2, arrived, 0)
    for copy in sides:
        copy.wait_recv()
    lax.fori_loop(0, 18, blend, 0)
    copies = finish(0)
    lax.fori_loop(SOLVES - 1, SOLVES, solve, 0)
    lax.fori_loop(SOLVES - 2, SOLVES, arrived, 0)
    lax.fori_loop(18, 34, blend, 0)
    copies += finish(1)

    def departed(i, carry):
        for copy in rows_of(i):
            copy.wait_send()
        return carry

    lax.fori_loop(0, SOLVES, departed, 0)
    for copy in sides + deeps + halo_copies + rims:
        copy.wait_send()
    for copy in swaps.values():
        copy.wait_send()
    for copy in windows.values():
        copy.wait_send()
    for copy in copies:
        copy.wait()


def assimilate(*arrays):
    dma = pltpu.SemaphoreType.DMA
    vmem = pl.BlockSpec(memory_space=pltpu.VMEM)
    return pl.pallas_call(
        kernel,
        out_shape=jax.ShapeDtypeStruct((16, 4, 8, 1024), F32),
        in_specs=[vmem] * 4 + [pl.BlockSpec(memory_space=pltpu.SMEM)] + [vmem] * 5,
        out_specs=pl.BlockSpec(memory_space=pl.ANY),
        scratch_shapes=[
            pltpu.VMEM((16, 4, 8, 1024), F32),
            pltpu.VMEM((8, 1024), jnp.int32),
            pltpu.VMEM((4, 2, 2, 8, 1024), F32),
            pltpu.VMEM((16, 8, 1024), F32),
            pltpu.VMEM((16, 3, 8, 1024), F32),
            pltpu.VMEM((4, 8, 128), F32),
            pltpu.VMEM((3, 32, 128), F32),
            pltpu.VMEM((5, 64, 8, 256), F32),
            pltpu.VMEM((5, 4, 8, 128), F32),
            pltpu.VMEM((5, 3, 32, 128), F32),
            pltpu.VMEM((64, 3, 8, 256), F32),
            pltpu.VMEM((4, 34, 64, 128), F32),
            pltpu.VMEM((264, 5, 8, 128), F32),
            pltpu.VMEM((64, 8, 128), F32),
            pltpu.VMEM((40, 384), F32),
            pltpu.VMEM((4, 40, 128), F32),
            pltpu.VMEM((32, 8, 128), jnp.int32),
            pltpu.VMEM((46, 8, 128), F32),
            pltpu.VMEM((45, 8, 128), F32),
            pltpu.VMEM((GROUP, 64, 128), F32),
            pltpu.VMEM((GROUP, 8, 128), F32),
            pltpu.VMEM((SPAN, 4, 8, 128), F32),
            pltpu.VMEM((SPAN * 16, 256), BF16),
            pltpu.VMEM((SPAN * 8, 256), BF16),
            pltpu.VMEM((SPAN * 8, 256), BF16),
            pltpu.VMEM((SPAN, 4, 8, 128), F32),
            pltpu.VMEM((64, 4, 8, 256), F32),
            dma((8,)), dma((8,)), dma((2,)), dma((2,)), dma((4,)), dma((4,)),
            dma((9,)), dma((12,)), dma((12,)), dma((3,)), dma((3,)),
            dma((64,)), dma((64,)), dma((4,)), dma((4,)),
            dma((3,)), dma((3,)), dma((2, SOLVES)), dma((2, SOLVES)),
            dma((4,)), dma((4,)), dma((4,)), dma((4,)), dma((6,)), dma((6,)),
        ],
        compiler_params=pltpu.CompilerParams(
            collective_id=0, has_side_effects=True, vmem_limit_bytes=LIMIT
        ),
    )(*arrays)


def body(
    trials_initial_dye,
    diffusivity,
    wet_mask,
    deeper_donor_tier,
    shallower_tier_fraction,
    obs_pos,
    obs_value,
    obs_var,
    observation_list,
    obs_count,
):
    return assimilate(
        trials_initial_dye,
        wet_mask,
        deeper_donor_tier,
        shallower_tier_fraction,
        diffusivity,
        obs_pos.reshape(64, 128),
        obs_value.reshape(64, 128),
        obs_var.reshape(64, 128),
        observation_list.reshape(128, 32),
        obs_count,
    )


def solution(mesh):
    return jax.shard_map(
        body,
        mesh=mesh,
        in_specs=(
            P("task", None, "patch", None),
            P(),
            P("patch", None),
            P(None, "patch", None),
            P(None, "patch", None),
            P("patch"),
            P("patch"),
            P("patch"),
            P("patch", "task", None),
            P("patch", "task"),
        ),
        out_specs=P("task", None, "patch", None),
        check_vma=False,
    )
```

```python
import functools

import jax
import jax.numpy as jnp
from jax import lax
from jax.experimental import pallas as pl
from jax.experimental.pallas import tpu as pltpu
from jax.sharding import PartitionSpec as P

MESH = pl.DeviceIdType.MESH
F32 = jnp.float32
BF16 = jnp.bfloat16
STEPS = 4
NS_ITERS = 6
TASKS = 4
STRIPS = 32
GROUP = 8
SPAN = 276
SOLVES = 64 // GROUP
LIMIT = 60 * 1024 * 1024


def iota(shape, dim):
    return lax.broadcasted_iota(jnp.int32, shape, dim)


def split(x):
    hi = x.astype(BF16)
    return hi, (x - hi.astype(F32)).astype(BF16)


def greet(peers):
    barrier = pltpu.get_barrier_semaphore()
    for peer in peers:
        pl.semaphore_signal(barrier, inc=1, device_id=peer, device_id_type=MESH)
    pl.semaphore_wait(barrier, len(peers))


def sender(src, dst, ss, rs, to):
    return pltpu.make_async_remote_copy(
        src_ref=src, dst_ref=dst, send_sem=ss, recv_sem=rs, device_id=to, device_id_type=MESH
    )


def spread(x, shift):
    lane = iota(x.shape, 1)
    return jnp.where(
        lane < 64, pltpu.roll(x, (127 - shift) % 128, 1), pltpu.roll(x, 63 - shift, 1)
    )


def beside(x):
    hi, lo = split(x)
    return jnp.concatenate([hi, lo], axis=1)


def doubled(both):
    left = jnp.where(iota((64, 128), 1) < 64, 1.0, 0.0)
    left, right = left.astype(BF16), (1.0 - left).astype(BF16)
    hi, lo = both[:, :128], both[:, 128:]
    hi = jnp.concatenate([hi * left, hi * right], axis=0)
    lo = jnp.concatenate([lo * left, lo * right], axis=0)
    return jnp.concatenate(
        [
            jnp.concatenate([hi, lo], axis=1),
            jnp.concatenate([hi, jnp.zeros((128, 128), BF16)], axis=1),
        ],
        axis=0,
    )


def times(both, weights):
    product = jnp.dot(both, weights, preferred_element_type=F32)
    return product[:, :128] + product[:, 128:]


def hat(x):
    return jnp.maximum(1.0 - jnp.abs(x - 1.5) * 0.25, 0.0)


def kernel(
    x, wet, donor, frac, rate, pos, value, var, listed, live,
    out,
    hal, whal, mixing, ring, fs0, fs1, es, attr,
    w5, e5, attr5, f1,
    every, cols, rim, mean, picked, base, taper, force, system, drive,
    turned, mid, top, low, total, result,
    halo_s, halo_r, wet_s, wet_r, attr_s, attr_r, own, swap_s, swap_r, rim_s, rim_r,
    win_s, win_r, edge_s, edge_r,
    deep_s, deep_r, row_s, row_r, side_s, side_r, corner_s, corner_r, back_s, back_r,
):
    t = lax.axis_index("task")
    s = lax.axis_index("patch")
    strip = {d: lax.rem(s + d + STRIPS, STRIPS) for d in (-2, -1, 1, 2)}
    up, down = strip[-1], strip[1]
    peer = {k: lax.rem(t + k, TASKS) for k in range(TASKS)}
    beyond = ((peer[1], 31, 0), (peer[3], 0, 33))
    way = 1 - 2 * lax.rem(s, 2)
    mate = s + way
    second = lax.rem(s + 2 * way + STRIPS, STRIPS)
    other = lax.rem(s - way + STRIPS, STRIPS)
    greet(
        [(t, strip[d]) for d in (-2, -1, 1, 2)]
        + [(peer[k], s) for k in (1, 2, 3)]
        + [(peer[k], y) for k in (1, 3) for y in (up, down)]
    )

    def send(src, dst, ss, rs, to):
        copy = sender(src, dst, ss, rs, to)
        copy.start()
        return copy

    wet_copies = []
    halo_copies = []
    for i, d in enumerate((-1, 1)):
        part = pl.ds(4 * i, 4)
        wet_copies.append(
            send(wet.at[part], whal.at[part], wet_s.at[i], wet_r.at[i], (t, strip[d]))
        )
    for c in range(4):
        members = pl.ds(4 * c, 4)
        for i, d in enumerate((-1, 1)):
            part = pl.ds(4 * i, 4)
            halo_copies.append(
                send(
                    x.at[members, :, part],
                    hal.at[members, :, part],
                    halo_s.at[2 * c + i],
                    halo_r.at[2 * c + i],
                    (t, strip[d]),
                )
            )

    facts = jnp.concatenate(
        [(pos[...] // 1024).astype(F32).T, value[...].T, var[...].T], axis=0
    )
    spot = iota((64, 128), 0)
    coarse = iota((64, 128), 1) - 1
    gathered = jnp.zeros((96, 128), F32)
    for m in range(4):
        taken = (spot == (coarse + 4) // 4 - 1 + 16 * t) & ((coarse + 4) % 4 == m)
        rows = jnp.concatenate([facts[128 * i + 32 * m : 128 * i + 32 * m + 32] for i in range(3)])
        gathered = gathered + jnp.dot(
            rows,
            jnp.where(taken, 1.0, 0.0),
            precision=lax.Precision.HIGHEST,
            preferred_element_type=F32,
        )
    lane96 = iota((32, 128), 1)
    known = (lane96 - 1 + 64 * t >= 0) & (lane96 - 1 + 64 * t < 256)
    attr[0] = gathered[0:32]
    attr[1] = gathered[32:64]
    attr[2] = jnp.where(known, gathered[64:96], 1.0)
    attr_copies = [
        send(attr, attr5.at[2 - d], attr_s.at[i], attr_r.at[i], (t, strip[d]))
        for i, d in enumerate((-2, -1, 1, 2))
    ]
    own_attr = pltpu.make_async_copy(attr, attr5.at[2], own.at[0])
    own_attr.start()

    sub = iota((8, 128), 0)
    lane = iota((8, 128), 1)
    below = jnp.where(s < STRIPS - 1, 1.0, 0.0)
    above = jnp.where(s > 0, 1.0, 0.0)
    inside = jnp.where(sub < 4, below, above)
    for copy in wet_copies:
        copy.wait()
    ocean = wet[...].astype(F32)
    ocean_halo = whal[...].astype(F32) * jnp.where(iota((8, 1024), 0) < 4, below, above)
    for lev in range(4):
        for i, mask in enumerate((ocean, ocean_halo)):
            mixing[lev, i, 0] = mask * (1.0 - 4.0 * rate[lev])
            mixing[lev, i, 1] = mask * rate[lev]
    es[...] = jnp.zeros_like(es)

    def advance(x, lev, which, row):
        fresh = []
        east = [pltpu.roll(a, 127, 1) for a in x] + [jnp.zeros((8, 128), F32)]
        west = [jnp.zeros((8, 128), F32)] + [pltpu.roll(a, 1, 1) for a in x]
        for j in range(8):
            around = (
                ring[lev, j, row + 1 : row + 9, :]
                + ring[lev, j, row - 1 : row + 7, :]
                + jnp.where(lane == 127, east[j + 1], east[j])
                + jnp.where(lane == 0, west[j], west[j + 1])
            )
            here = slice(128 * j, 128 * j + 128)
            fresh.append(
                mixing[lev, which, 0, :, here] * x[j] + mixing[lev, which, 1, :, here] * around
            )
        return fresh

    def member(m, carry):
        levels = [
            [x[m, lev, :, 128 * j : 128 * j + 128] for j in range(8)] for lev in range(4)
        ]
        rests = [
            [hal[m, lev, :, 128 * j : 128 * j + 128] * inside for j in range(8)]
            for lev in range(4)
        ]
        for step in range(STEPS):
            for lev in range(4):
                for j in range(8):
                    ring[lev, j, 0:8, :] = rests[lev][j]
                    ring[lev, j, 8:16, :] = levels[lev][j]
                    ring[lev, j, 16:24, :] = rests[lev][j]
                    ring[lev, j, 24:32, :] = levels[lev][j]
            for lev in range(4):
                levels[lev] = advance(levels[lev], lev, 0, 8)
                if step < STEPS - 1:
                    rests[lev] = advance(rests[lev], lev, 1, 16)
        surface = []
        for j in range(8):
            here = slice(128 * j, 128 * j + 128)
            for lev in range(4):
                tier = donor[lev, :, here]
                first, second = tier == 0, tier == 1
                one, two, three, four = (levels[i][j] for i in range(4))
                near = jnp.where(first, one, jnp.where(second, two, three))
                far = jnp.where(first, two, jnp.where(second, three, four))
                share = frac[lev, :, here]
                mixed = (1.0 - share) * near + share * far
                if lev:
                    fs1[m, lev - 1, :, here] = mixed
                else:
                    fs0[m, :, here] = mixed
                    surface.append(mixed)
        for k in range(TASKS):
            edge = jnp.where(lane >= 124, surface[(2 * k - 1) % 8], surface[(2 * k + 2) % 8])
            es[k] = jnp.where(lane // 8 == m, pltpu.roll(edge, m * 8 + 4, 1), es[k])
        return carry

    here_cols = pl.ds(pl.multiple_of(256 * t, 256), 256)
    local, own_deeps, deeps = [], [], []
    swaps = {}
    windows = {}

    def block(src, c):
        return pl.ds(pl.multiple_of(16 * src + 4 * c, 4), 4)

    def exchange(c):
        chunk = pl.ds(4 * c, 4)
        copy = pltpu.make_async_copy(
            fs0.at[chunk, :, here_cols], w5.at[2, block(t, c)], own.at[1 + c]
        )
        copy.start()
        local.append(copy)
        for k in (1, 2, 3):
            to = peer[k]
            cols = pl.ds(pl.multiple_of(256 * to, 256), 256)
            i = 3 * c + k - 1
            swaps[c, k] = send(
                fs0.at[chunk, :, cols], w5.at[2, block(t, c)], swap_s.at[i], swap_r.at[i], (to, s)
            )
        copy = pltpu.make_async_copy(
            fs1.at[chunk, :, :, here_cols], f1.at[block(t, c)], own.at[9 + c]
        )
        copy.start()
        own_deeps.append(copy)
        for k in (1, 2, 3):
            to = peer[k]
            cols = pl.ds(pl.multiple_of(256 * to, 256), 256)
            i = 3 * c + k - 1
            deeps.append(
                send(
                    fs1.at[chunk, :, :, cols], f1.at[block(t, c)],
                    deep_s.at[i], deep_r.at[i], (to, s),
                )
            )

    def forward(c):
        for k in range(TASKS):
            src = lax.rem(t - k + TASKS, TASKS)
            part = block(src, c)
            if k:
                swaps[c, k].wait_recv()
                held = w5.at[2, part]
            else:
                held = fs0.at[pl.ds(4 * c, 4), :, here_cols]
            for j, (to, slot) in enumerate(
                ((other, 2 + way), (second, 2 - 2 * way), (mate, 2 - way))
            ):
                i = 16 * j + 4 * c + k
                windows[j, c, k] = send(
                    held, w5.at[slot, part], win_s.at[i], win_r.at[i], (t, to)
                )

    def relay(c):
        for k in range(TASKS):
            src = lax.rem(t - k + TASKS, TASKS)
            part = block(src, c)
            windows[0, c, k].wait_recv()
            i = 48 + 4 * c + k
            windows[3, c, k] = send(
                w5.at[2 - way, part], w5.at[2 - 2 * way, part],
                win_s.at[i], win_r.at[i], (t, mate),
            )

    for c in range(4):
        halo_copies[2 * c].wait_recv()
        halo_copies[2 * c + 1].wait_recv()
        lax.fori_loop(4 * c, 4 * c + 4, member, 0)
        exchange(c)
        if c == 3:
            rims = []
            for k in (1, 2, 3):
                rims.append(
                    send(
                        es.at[peer[k]], e5.at[2, t], rim_s.at[k - 1], rim_r.at[k - 1], (peer[k], s)
                    )
                )
            own_rim = pltpu.make_async_copy(es.at[t], e5.at[2, t], own.at[5])
            own_rim.start()
        if c:
            forward(c - 1)
    forward(3)
    own_rim.wait()
    for copy in rims:
        copy.wait_recv()
    edges = [
        send(e5.at[2], e5.at[2 - d], edge_s.at[i], edge_r.at[i], (t, strip[d]))
        for i, d in enumerate((-2, -1, 1, 2))
    ]
    mine = pl.ds(pl.multiple_of(16 * t, 16), 16)

    def place(st):
        for src in range(TASKS):
            tile = e5[st, src]
            for m in range(16):
                rim[16 * src + m] = pltpu.roll(tile, (128 - 8 * m) % 128, 1) if m else tile
        rows = pl.ds(pl.multiple_of(8 * st, 8), 8)
        means, rim_means = [], []
        for r in range(8):
            whole = w5[st, :, r, :]
            mu = jnp.sum(whole, axis=0, keepdims=True) * (1.0 / 64)
            dev = whole - mu
            cols[4:260, st, r, :] = jnp.concatenate([dev, dev], axis=0).T
            means.append(mu)
            whole = rim[:, r, :]
            mu = jnp.sum(whole, axis=0, keepdims=True) * (1.0 / 64)
            dev = whole - mu
            turned = jnp.concatenate([dev, dev], axis=0).T
            cols[0:4, st, r, :] = turned[0:4]
            cols[260:264, st, r, :] = turned[4:8]
            rim_means.append(mu)
        mean[rows, 0:256] = jnp.concatenate(means, axis=0)
        mean[rows, 256:384] = jnp.concatenate(rim_means, axis=0)

    for copy in local:
        copy.wait()
    place(2)
    flat = jnp.concatenate([listed[0], listed[1]], axis=1)
    block_col = 4 * (iota((32, 128), 1) % 64) + 256 * t - 4
    code = ((flat // 8192 - (s - 2)) * 9 + flat % 8192 // 8 - block_col) * 8 + flat % 8
    pick = iota((64, 128), 0)
    into = iota((64, 128), 1)
    counts = live[...].astype(F32)
    alive = jnp.dot(
        counts, jnp.where(pick == into, 1.0, 0.0), preferred_element_type=F32
    )[0:1] + jnp.dot(counts, jnp.where(pick == into - 64, 1.0, 0.0), preferred_element_type=F32)[1:2]
    for slot in range(32):
        kept = jnp.where(alive > slot, code[slot : slot + 1, :], -100000)
        base[slot] = jnp.broadcast_to(kept, (8, 128)) - sub

    for copy in attr_copies:
        copy.wait()
    own_attr.wait()
    point_row = jnp.where(lane < 64, 1.5, 5.5)
    height = sub.astype(F32)
    taper[45] = jnp.zeros((8, 128), F32)

    def weigh(st, carry):
        for cr in range(9):
            q, shift = (cr - 4) % 4, (cr - 4) // 4
            row = spread(attr5[st, 0, 8 * q : 8 * q + 8, :], shift)
            value = spread(attr5[st, 1, 8 * q : 8 * q + 8, :], shift)
            var = spread(attr5[st, 2, 8 * q : 8 * q + 8, :], shift)
            tile = (st * 9 + cr) * 8
            count = jnp.zeros((8, 128), F32)
            for slot in range(32):
                count = count + jnp.where(base[slot] == tile, 1.0, 0.0)
            apart = row + (8.0 * (st - 2).astype(F32)) - point_row
            dist = apart * apart + (cr - 5.5) ** 2
            weight = count * jnp.exp(dist * (-1.0 / 1152.0)) / var
            pull = weight * value
            held = jnp.zeros((8, 128), F32)
            pulled = jnp.zeros((8, 128), F32)
            for k in range(8):
                hit = row[k : k + 1] == height
                held = held + jnp.where(hit, weight[k : k + 1], 0.0)
                pulled = pulled + jnp.where(hit, pull[k : k + 1], 0.0)
            taper[cr * 5 + st] = held
            force[cr * 5 + st] = pulled
        return carry

    lax.fori_loop(0, 5, weigh, 0)

    def field(lev, r):
        return w5[2, :, r, :] if lev == 0 else f1[:, lev - 1, r, :]

    def turn(lev):
        for r in range(8):
            whole = field(lev, r)
            dev = whole - jnp.sum(whole, axis=0, keepdims=True) * (1.0 / 64)
            turned[10:266, r // 2, 4 * (r % 2) + lev, :] = jnp.concatenate([dev, dev], axis=0).T

    total[...] = jnp.zeros_like(total)
    for ref in (mid, top, low):
        ref[...] = jnp.zeros_like(ref)
    turn(0)

    row = iota((8, 128), 0) // 4
    offset = jnp.where(lane < 64, 0.0, 4.0)
    first_strip = jnp.where(s == 0, 1.0, 0.0)
    last_strip = jnp.where(s == STRIPS - 1, 1.0, 0.0)

    def row_share(a, k):
        r = (2 * k + row).astype(F32)
        if a == -1:
            return hat(r + 4.0) * (1.0 - first_strip)
        if a == 0:
            return hat(r) + hat(r + 4.0) * first_strip
        if a == 1:
            return hat(r - 4.0) + hat(r - 8.0) * last_strip
        return hat(r - 8.0) * (1.0 - last_strip)

    left = iota((8, 8, 128), 2) < 64

    def parted(x, share):
        x = x * share[None]
        high = x.astype(BF16).astype(F32)
        return jnp.where(left, high, x - high)

    def part(n, carry):
        for k, a, ref in ((0, -1, top), (3, 1, low)):
            x = turned[pl.ds(8 * n + 10, 8), k]
            both = jnp.concatenate(
                [parted(x, row_share(a, k)), parted(x, row_share(a + 1, k))], axis=2
            )
            ref[pl.ds(pl.multiple_of(64 * n + 80, 16), 64)] = both.reshape(64, 256).astype(BF16)
        pieces = []
        for k in (1, 2):
            x = turned[pl.ds(8 * n + 10, 8), k]
            pieces.append(
                jnp.concatenate([parted(x, row_share(0, k)), parted(x, row_share(1, k))], axis=2)
            )
        both = jnp.stack(pieces, axis=1)
        mid[pl.ds(pl.multiple_of(128 * n + 160, 16), 128)] = both.reshape(128, 256).astype(BF16)
        return carry

    relay(0)
    relay(1)
    for copy in edges:
        copy.wait()
    for c in range(4):
        for k in range(TASKS):
            windows[2, c, k].wait_recv()
    place(2 + way)
    for copy in own_deeps:
        copy.wait()
    for copy in deeps:
        copy.wait_recv()
    for lev in (1, 2, 3):
        turn(lev)
    relay(2)
    lax.fori_loop(0, 32, part, 0)
    relay(3)
    place(2 - way)
    for j, slot in ((1, 2 - 2 * way), (3, 2 + 2 * way)):
        for c in range(4):
            for k in range(TASKS):
                windows[j, c, k].wait_recv()
        place(slot)

    spot = iota((384, 128), 0)
    coarse = iota((384, 128), 1)
    lane_of = iota((40, 384), 1)
    known = jnp.where(lane_of < 264, mean[...], 0.0)
    for q in range(4):
        want = jnp.where(
            coarse == 0, 256 + q, jnp.where(coarse == 65, 260 + q, 4 * coarse - 4 + q)
        )
        picked[q] = jnp.dot(
            known,
            jnp.where((spot == want) & (coarse < 66), 1.0, 0.0),
            precision=lax.Precision.HIGHEST,
            preferred_element_type=F32,
        )
    def recentre(st, carry):
        for cr in range(9):
            q, shift = (cr - 4) % 4, (cr - 4) // 4
            centre = spread(picked[q, pl.ds(pl.multiple_of(8 * st, 8), 8), :], shift)
            force[cr * 5 + st] = force[cr * 5 + st] - taper[cr * 5 + st] * centre
        return carry

    lax.fori_loop(0, 5, recentre, 0)

    tall_lane = iota((368, 128), 1)
    eye = jnp.where(iota((64, 128), 0) == iota((64, 128), 1) % 64, 1.0, 0.0)

    def gram(b):
        index = jnp.where(lane < 64, b, 64 + b)
        near = cols[pl.ds(4 * b, 10)].reshape(400, 128)[:368]
        spread_taper = jnp.concatenate(
            [jnp.take_along_axis(taper[k], index, axis=1) for k in range(46)], axis=0
        )
        spread_force = jnp.concatenate(
            [jnp.take_along_axis(force[k], index, axis=1) for k in range(45)], axis=0
        )
        s_hi, s_lo = split(near * spread_taper)
        n_hi = near.astype(BF16).astype(F32)
        both = jnp.where(tall_lane < 64, n_hi, near - n_hi).astype(BF16)
        product = lax.dot_general(
            both,
            jnp.concatenate([s_hi, s_lo], axis=1),
            (((0,), (0,)), ((), ())),
            preferred_element_type=F32,
        )
        product = product[:64] + product[64:]
        return (
            product[:, :128] + product[:, 128:] + 63.0 * eye,
            jnp.sum(near[:360] * spread_force, axis=0, keepdims=True),
        )

    def keep(k, made):
        system[k] = made[0]
        drive[k] = jnp.broadcast_to(made[1], (8, 128))

    for k in range(GROUP):
        keep(k, gram(64 - GROUP + k))

    half = iota((64, 128), 1) < 64

    def rows_of(i):
        n = lax.rem(i + SOLVES - 1, SOLVES)
        part = pl.ds(1 + n * (GROUP // 2), GROUP // 2)
        return [
            sender(
                every.at[1 + a, part], every.at[3 - 3 * a, part],
                row_s.at[a, i], row_r.at[a, i], (t, (up, down)[a]),
            )
            for a in range(2)
        ]

    def sides_of():
        copies = []
        for i, (to, at, there) in enumerate(beyond):
            for a in range(2):
                copies.append(
                    sender(
                        every.at[1 + a, at + 1], every.at[1 + a, there],
                        side_s.at[2 * i + a], side_r.at[2 * i + a], (to, s),
                    )
                )
                copies.append(
                    sender(
                        every.at[1 + a, at + 1], every.at[3 - 3 * a, there],
                        corner_s.at[2 * i + a], corner_r.at[2 * i + a], (to, (up, down)[a]),
                    )
                )
        return copies

    def solve(i, carry):
        n = lax.rem(i + SOLVES - 1, SOLVES)
        nears, inverses, norms = [], [], []
        systems = [system[k] for k in range(GROUP)]
        drives = [drive[k][:1] for k in range(GROUP)]
        later = jnp.minimum(i, SOLVES - 2) * GROUP
        made = []

        def share(n):
            for k in range(n * GROUP // (2 * NS_ITERS), (n + 1) * GROUP // (2 * NS_ITERS)):
                made.append(gram(later + k))

        for x in systems:
            squares = jnp.sum(x * x, axis=0, keepdims=True)
            left = iota((1, 128), 1) < 64
            one = jnp.sum(jnp.where(left, squares, 0.0), axis=1, keepdims=True)
            two = jnp.sum(jnp.where(left, 0.0, squares), axis=1, keepdims=True)
            norm = jnp.sqrt(jnp.where(left, one, two))
            norms.append(norm)
            nears.append(x / norm)
            inverses.append(None)
        for turn in range(NS_ITERS):
            share(2 * turn)
            parts = [beside(x) for x in nears]
            weights = [doubled(x) for x in parts]
            if turn == 0:
                inverses = [1.5 * eye - 0.5 * x for x in nears]
                squared = [times(x, y) for x, y in zip(parts, weights)]
            elif turn < NS_ITERS - 1:
                squared = []
                for k in range(GROUP):
                    product = times(
                        jnp.concatenate([parts[k], beside(inverses[k])], axis=0), weights[k]
                    )
                    squared.append(product[:64])
                    inverses[k] = 1.5 * inverses[k] - 0.5 * product[64:]
            else:
                inverses = [
                    1.5 * x - 0.5 * times(beside(x), y) for x, y in zip(inverses, weights)
                ]
            share(2 * turn + 1)
            if turn < NS_ITERS - 1:
                nears = [
                    2.25 * x - 1.5 * y + 0.25 * times(beside(y), z)
                    for x, y, z in zip(nears, squared, weights)
                ]

        def standing(x):
            one = jnp.sum(jnp.where(half, x, 0.0), axis=1, keepdims=True)
            two = jnp.sum(jnp.where(half, 0.0, x), axis=1, keepdims=True)
            return jnp.where(half, one, two)

        finals = []
        for k in range(GROUP):
            z = inverses[k]
            once = jnp.sum(z * standing(eye * drives[k]), axis=0, keepdims=True)
            drift = standing(z * (once / norms[k]))
            finals.append(jnp.sqrt(63.0 / norms[k]) * z + drift)
        for k in range(0, GROUP, 2):
            g = n * (GROUP // 2) + k // 2
            every[1, g + 1] = jnp.where(half, finals[k], pltpu.roll(finals[k + 1], 64, 1))
            every[2, g + 1] = jnp.where(half, pltpu.roll(finals[k], 64, 1), finals[k + 1])
        for k in range(GROUP):
            keep(k, made[k])
        for copy in rows_of(i):
            copy.start()

        @pl.when(i == 1)
        def _():
            for copy in sides_of():
                copy.start()

        return carry

    def col_share(g):
        first = jnp.where((g == 0) & (t == 0), 1.0, 0.0)
        last = jnp.where((g == 31) & (t == TASKS - 1), 1.0, 0.0)
        alive = jnp.where(
            ((g == -1) & (t == 0)) | ((g == 32) & (t == TASKS - 1)), 0.0, 1.0
        )
        shares = []
        for c in range(12):
            x = (c - 2.0) - offset
            share = hat(x)
            if c in (2, 3):
                share = share + jnp.where(lane < 64, hat(x + 4.0), 0.0) * first
            if c in (8, 9):
                share = share + jnp.where(lane < 64, 0.0, hat(x - 4.0)) * last
            shares.append(share * alive)
        return shares

    def paired(x):
        hi, lo = split(x)
        zero = jnp.zeros((64, 128), BF16)
        return jnp.concatenate(
            [jnp.concatenate([hi, lo], axis=1), jnp.concatenate([hi, zero], axis=1)], axis=0
        )

    def blend(n, carry):
        g = n - 1
        shares = col_share(g)
        operands = [paired(every[a, n]) for a in range(4)]
        for a, ref, height, first in ((0, top, 8, 0), (1, mid, 16, 1), (2, low, 8, 3)):
            rows = ref[pl.ds(pl.multiple_of(height * (8 * g + 8), 16), 12 * height)]
            product = jnp.dot(
                rows,
                jnp.concatenate([operands[a], operands[a + 1]], axis=0),
                preferred_element_type=F32,
            )
            product = (product[:, :128] + product[:, 128:]).reshape(12, height // 8, 8, 128)
            for c in range(12):
                total[8 * g + 8 + c, first : first + height // 8] += product[c] * shares[c][None]
        return carry

    def finish(h):
        copies = []
        here = slice(128 * h, 128 * h + 128)
        ocean_cols = pl.ds(pl.multiple_of(256 * t + 128 * h, 128), 128)
        for r in range(8):
            ocean = wet[r : r + 1, ocean_cols].astype(F32)
            for lev in range(4):
                back = total[10 + 128 * h : 138 + 128 * h, r // 2, 4 * (r % 2) + lev, :].T
                whole = field(lev, r)[:, here]
                dev = whole - jnp.sum(whole, axis=0, keepdims=True) * (1.0 / 64)
                result[:, lev, r, here] = whole + ocean * (back[:64] + back[64:] - dev)
        copy = pltpu.make_async_copy(
            result.at[mine, :, :, here], out.at[:, :, :, ocean_cols], own.at[7 + h]
        )
        copy.start()
        copies.append(copy)
        for k in (1, 2, 3):
            theirs = pl.ds(pl.multiple_of(16 * peer[k], 16), 16)
            copies.append(
                send(
                    result.at[theirs, :, :, here], out.at[:, :, :, ocean_cols],
                    back_s.at[3 * h + k - 1], back_r.at[3 * h + k - 1], (peer[k], s),
                )
            )
        return copies

    lax.fori_loop(0, SOLVES - 1, solve, 0)

    def arrived(i, carry):
        for copy in rows_of(i):
            copy.wait_recv()
        return carry

    sides = sides_of()
    lax.fori_loop(0, SOLVES - 2, arrived, 0)
    for copy in sides:
        copy.wait_recv()
    lax.fori_loop(0, 18, blend, 0)
    copies = finish(0)
    lax.fori_loop(SOLVES - 1, SOLVES, solve, 0)
    lax.fori_loop(SOLVES - 2, SOLVES, arrived, 0)
    lax.fori_loop(18, 34, blend, 0)
    copies += finish(1)

    def departed(i, carry):
        for copy in rows_of(i):
            copy.wait_send()
        return carry

    lax.fori_loop(0, SOLVES, departed, 0)
    for copy in sides + deeps + halo_copies + rims:
        copy.wait_send()
    for copy in swaps.values():
        copy.wait_send()
    for copy in windows.values():
        copy.wait_send()
    for copy in copies:
        copy.wait()


def assimilate(*arrays):
    dma = pltpu.SemaphoreType.DMA
    vmem = pl.BlockSpec(memory_space=pltpu.VMEM)
    return pl.pallas_call(
        kernel,
        out_shape=jax.ShapeDtypeStruct((16, 4, 8, 1024), F32),
        in_specs=[vmem] * 4 + [pl.BlockSpec(memory_space=pltpu.SMEM)] + [vmem] * 5,
        out_specs=pl.BlockSpec(memory_space=pl.ANY),
        scratch_shapes=[
            pltpu.VMEM((16, 4, 8, 1024), F32),
            pltpu.VMEM((8, 1024), jnp.int32),
            pltpu.VMEM((4, 2, 2, 8, 1024), F32),
            pltpu.VMEM((4, 8, 32, 128), F32),
            pltpu.VMEM((16, 8, 1024), F32),
            pltpu.VMEM((16, 3, 8, 1024), F32),
            pltpu.VMEM((4, 8, 128), F32),
            pltpu.VMEM((3, 32, 128), F32),
            pltpu.VMEM((5, 64, 8, 256), F32),
            pltpu.VMEM((5, 4, 8, 128), F32),
            pltpu.VMEM((5, 3, 32, 128), F32),
            pltpu.VMEM((64, 3, 8, 256), F32),
            pltpu.VMEM((4, 34, 64, 128), F32),
            pltpu.VMEM((264, 5, 8, 128), F32),
            pltpu.VMEM((64, 8, 128), F32),
            pltpu.VMEM((40, 384), F32),
            pltpu.VMEM((4, 40, 128), F32),
            pltpu.VMEM((32, 8, 128), jnp.int32),
            pltpu.VMEM((46, 8, 128), F32),
            pltpu.VMEM((45, 8, 128), F32),
            pltpu.VMEM((GROUP, 64, 128), F32),
            pltpu.VMEM((GROUP, 8, 128), F32),
            pltpu.VMEM((SPAN, 4, 8, 128), F32),
            pltpu.VMEM((SPAN * 16, 256), BF16),
            pltpu.VMEM((SPAN * 8, 256), BF16),
            pltpu.VMEM((SPAN * 8, 256), BF16),
            pltpu.VMEM((SPAN, 4, 8, 128), F32),
            pltpu.VMEM((64, 4, 8, 256), F32),
            dma((8,)), dma((8,)), dma((2,)), dma((2,)), dma((4,)), dma((4,)),
            dma((13,)), dma((12,)), dma((12,)), dma((3,)), dma((3,)),
            dma((64,)), dma((64,)), dma((4,)), dma((4,)),
            dma((12,)), dma((12,)), dma((2, SOLVES)), dma((2, SOLVES)),
            dma((4,)), dma((4,)), dma((4,)), dma((4,)), dma((6,)), dma((6,)),
        ],
        compiler_params=pltpu.CompilerParams(
            collective_id=0, has_side_effects=True, vmem_limit_bytes=LIMIT
        ),
    )(*arrays)


def body(
    trials_initial_dye,
    diffusivity,
    wet_mask,
    deeper_donor_tier,
    shallower_tier_fraction,
    obs_pos,
    obs_value,
    obs_var,
    observation_list,
    obs_count,
):
    return assimilate(
        trials_initial_dye,
        wet_mask,
        deeper_donor_tier,
        shallower_tier_fraction,
        diffusivity,
        obs_pos.reshape(64, 128),
        obs_value.reshape(64, 128),
        obs_var.reshape(64, 128),
        observation_list.transpose(0, 2, 1),
        obs_count,
    )


def solution(mesh):
    return jax.shard_map(
        body,
        mesh=mesh,
        in_specs=(
            P("task", None, "patch", None),
            P(),
            P("patch", None),
            P(None, "patch", None),
            P(None, "patch", None),
            P("patch"),
            P("patch"),
            P("patch"),
            P("patch", "task", None),
            P("patch", "task"),
        ),
        out_specs=P("task", None, "patch", None),
        check_vma=False,
    )
```

```python
import functools

import jax
import jax.numpy as jnp
from jax import lax
from jax.experimental import pallas as pl
from jax.experimental.pallas import tpu as pltpu
from jax.sharding import PartitionSpec as P

MESH = pl.DeviceIdType.MESH
F32 = jnp.float32
BF16 = jnp.bfloat16
STEPS = 4
NS_ITERS = 6
TASKS = 4
STRIPS = 32
GROUP = 8
SPAN = 276
SOLVES = 64 // GROUP
LIMIT = 60 * 1024 * 1024


def iota(shape, dim):
    return lax.broadcasted_iota(jnp.int32, shape, dim)


def split(x):
    hi = x.astype(BF16)
    return hi, (x - hi.astype(F32)).astype(BF16)


def greet(peers):
    barrier = pltpu.get_barrier_semaphore()
    for peer in peers:
        pl.semaphore_signal(barrier, inc=1, device_id=peer, device_id_type=MESH)
    pl.semaphore_wait(barrier, len(peers))


def sender(src, dst, ss, rs, to):
    return pltpu.make_async_remote_copy(
        src_ref=src, dst_ref=dst, send_sem=ss, recv_sem=rs, device_id=to, device_id_type=MESH
    )


def spread(x, shift):
    lane = iota(x.shape, 1)
    return jnp.where(
        lane < 64, pltpu.roll(x, (127 - shift) % 128, 1), pltpu.roll(x, 63 - shift, 1)
    )


def beside(x):
    hi, lo = split(x)
    return jnp.concatenate([hi, lo], axis=1)


def doubled(both):
    left = jnp.where(iota((64, 128), 1) < 64, 1.0, 0.0)
    left, right = left.astype(BF16), (1.0 - left).astype(BF16)
    hi, lo = both[:, :128], both[:, 128:]
    hi = jnp.concatenate([hi * left, hi * right], axis=0)
    lo = jnp.concatenate([lo * left, lo * right], axis=0)
    return jnp.concatenate(
        [
            jnp.concatenate([hi, lo], axis=1),
            jnp.concatenate([hi, jnp.zeros((128, 128), BF16)], axis=1),
        ],
        axis=0,
    )


def times(both, weights):
    product = jnp.dot(both, weights, preferred_element_type=F32)
    return product[:, :128] + product[:, 128:]


def hat(x):
    return jnp.maximum(1.0 - jnp.abs(x - 1.5) * 0.25, 0.0)


def kernel(
    x, wet, donor, frac, rate, pos, value, var, listed, live,
    out,
    hal, whal, mixing, ring, fs0, fs1, es, attr,
    w5, e5, attr5, f1,
    every, cols, rim, mean, picked, base, taper, force, system, drive,
    turned, mid, top, low, total, result,
    halo_s, halo_r, wet_s, wet_r, attr_s, attr_r, own, swap_s, swap_r, rim_s, rim_r,
    win_s, win_r, edge_s, edge_r,
    deep_s, deep_r, row_s, row_r, side_s, side_r, corner_s, corner_r, back_s, back_r,
):
    t = lax.axis_index("task")
    s = lax.axis_index("patch")
    strip = {d: lax.rem(s + d + STRIPS, STRIPS) for d in (-2, -1, 1, 2)}
    up, down = strip[-1], strip[1]
    peer = {k: lax.rem(t + k, TASKS) for k in range(TASKS)}
    beyond = ((peer[1], 31, 0), (peer[3], 0, 33))
    way = 1 - 2 * lax.rem(s, 2)
    mate = s + way
    second = lax.rem(s + 2 * way + STRIPS, STRIPS)
    other = lax.rem(s - way + STRIPS, STRIPS)
    greet(
        [(t, strip[d]) for d in (-2, -1, 1, 2)]
        + [(peer[k], s) for k in (1, 2, 3)]
        + [(peer[k], y) for k in (1, 3) for y in (up, down)]
    )

    def send(src, dst, ss, rs, to):
        copy = sender(src, dst, ss, rs, to)
        copy.start()
        return copy

    wet_copies = []
    halo_copies = []
    for i, d in enumerate((-1, 1)):
        part = pl.ds(4 * i, 4)
        wet_copies.append(
            send(wet.at[part], whal.at[part], wet_s.at[i], wet_r.at[i], (t, strip[d]))
        )
    for c in range(4):
        members = pl.ds(4 * c, 4)
        for i, d in enumerate((-1, 1)):
            part = pl.ds(4 * i, 4)
            halo_copies.append(
                send(
                    x.at[members, :, part],
                    hal.at[members, :, part],
                    halo_s.at[2 * c + i],
                    halo_r.at[2 * c + i],
                    (t, strip[d]),
                )
            )

    facts = jnp.concatenate(
        [(pos[...] // 1024).astype(F32).T, value[...].T, var[...].T], axis=0
    )
    spot = iota((64, 128), 0)
    coarse = iota((64, 128), 1) - 1
    gathered = jnp.zeros((96, 128), F32)
    for m in range(4):
        taken = (spot == (coarse + 4) // 4 - 1 + 16 * t) & ((coarse + 4) % 4 == m)
        rows = jnp.concatenate([facts[128 * i + 32 * m : 128 * i + 32 * m + 32] for i in range(3)])
        gathered = gathered + jnp.dot(
            rows,
            jnp.where(taken, 1.0, 0.0),
            precision=lax.Precision.HIGHEST,
            preferred_element_type=F32,
        )
    lane96 = iota((32, 128), 1)
    known = (lane96 - 1 + 64 * t >= 0) & (lane96 - 1 + 64 * t < 256)
    attr[0] = gathered[0:32]
    attr[1] = gathered[32:64]
    attr[2] = jnp.where(known, gathered[64:96], 1.0)
    attr_copies = [
        send(attr, attr5.at[2 - d], attr_s.at[i], attr_r.at[i], (t, strip[d]))
        for i, d in enumerate((-2, -1, 1, 2))
    ]
    own_attr = pltpu.make_async_copy(attr, attr5.at[2], own.at[0])
    own_attr.start()

    sub = iota((8, 128), 0)
    lane = iota((8, 128), 1)
    below = jnp.where(s < STRIPS - 1, 1.0, 0.0)
    above = jnp.where(s > 0, 1.0, 0.0)
    inside = jnp.where(sub < 4, below, above)
    for copy in wet_copies:
        copy.wait()
    ocean = wet[...].astype(F32)
    ocean_halo = whal[...].astype(F32) * jnp.where(iota((8, 1024), 0) < 4, below, above)
    for lev in range(4):
        for i, mask in enumerate((ocean, ocean_halo)):
            mixing[lev, i, 0] = mask * (1.0 - 4.0 * rate[lev])
            mixing[lev, i, 1] = mask * rate[lev]
    es[...] = jnp.zeros_like(es)

    def advance(x, lev, which, row):
        fresh = []
        east = [pltpu.roll(a, 127, 1) for a in x] + [jnp.zeros((8, 128), F32)]
        west = [jnp.zeros((8, 128), F32)] + [pltpu.roll(a, 1, 1) for a in x]
        for j in range(8):
            around = (
                ring[lev, j, row + 1 : row + 9, :]
                + ring[lev, j, row - 1 : row + 7, :]
                + jnp.where(lane == 127, east[j + 1], east[j])
                + jnp.where(lane == 0, west[j], west[j + 1])
            )
            here = slice(128 * j, 128 * j + 128)
            fresh.append(
                mixing[lev, which, 0, :, here] * x[j] + mixing[lev, which, 1, :, here] * around
            )
        return fresh

    def member(m, carry):
        levels = [
            [x[m, lev, :, 128 * j : 128 * j + 128] for j in range(8)] for lev in range(4)
        ]
        rests = [
            [hal[m, lev, :, 128 * j : 128 * j + 128] * inside for j in range(8)]
            for lev in range(4)
        ]
        for step in range(STEPS):
            for lev in range(4):
                for j in range(8):
                    ring[lev, j, 0:8, :] = rests[lev][j]
                    ring[lev, j, 8:16, :] = levels[lev][j]
                    ring[lev, j, 16:24, :] = rests[lev][j]
                    ring[lev, j, 24:32, :] = levels[lev][j]
            for lev in range(4):
                levels[lev] = advance(levels[lev], lev, 0, 8)
                if step < STEPS - 1:
                    rests[lev] = advance(rests[lev], lev, 1, 16)
        surface = []
        for j in range(8):
            here = slice(128 * j, 128 * j + 128)
            for lev in range(4):
                tier = donor[lev, :, here]
                first, second = tier == 0, tier == 1
                one, two, three, four = (levels[i][j] for i in range(4))
                near = jnp.where(first, one, jnp.where(second, two, three))
                far = jnp.where(first, two, jnp.where(second, three, four))
                share = frac[lev, :, here]
                mixed = (1.0 - share) * near + share * far
                if lev:
                    fs1[m, lev - 1, :, here] = mixed
                else:
                    fs0[m, :, here] = mixed
                    surface.append(mixed)
        for k in range(TASKS):
            edge = jnp.where(lane >= 124, surface[(2 * k - 1) % 8], surface[(2 * k + 2) % 8])
            es[k] = jnp.where(lane // 8 == m, pltpu.roll(edge, m * 8 + 4, 1), es[k])
        return carry

    here_cols = pl.ds(pl.multiple_of(256 * t, 256), 256)
    local, own_deeps, deeps = [], [], []
    swaps = {}
    windows = {}

    def block(src, c):
        return pl.ds(pl.multiple_of(16 * src + 4 * c, 4), 4)

    def exchange(c):
        chunk = pl.ds(4 * c, 4)
        copy = pltpu.make_async_copy(
            fs0.at[chunk, :, here_cols], w5.at[2, block(t, c)], own.at[1 + c]
        )
        copy.start()
        local.append(copy)
        for k in (1, 2, 3):
            to = peer[k]
            cols = pl.ds(pl.multiple_of(256 * to, 256), 256)
            i = 3 * c + k - 1
            swaps[c, k] = send(
                fs0.at[chunk, :, cols], w5.at[2, block(t, c)], swap_s.at[i], swap_r.at[i], (to, s)
            )

    def deepen(c):
        chunk = pl.ds(4 * c, 4)
        copy = pltpu.make_async_copy(
            fs1.at[chunk, :, :, here_cols], f1.at[block(t, c)], own.at[9 + c]
        )
        copy.start()
        own_deeps.append(copy)
        for k in (1, 2, 3):
            to = peer[k]
            cols = pl.ds(pl.multiple_of(256 * to, 256), 256)
            i = 3 * c + k - 1
            deeps.append(
                send(
                    fs1.at[chunk, :, :, cols], f1.at[block(t, c)],
                    deep_s.at[i], deep_r.at[i], (to, s),
                )
            )

    def forward(c):
        for k in range(TASKS):
            src = lax.rem(t - k + TASKS, TASKS)
            part = block(src, c)
            if k:
                swaps[c, k].wait_recv()
                held = w5.at[2, part]
            else:
                held = fs0.at[pl.ds(4 * c, 4), :, here_cols]
            for j, (to, slot) in enumerate(
                ((other, 2 + way), (second, 2 - 2 * way), (mate, 2 - way))
            ):
                i = 16 * j + 4 * c + k
                windows[j, c, k] = send(
                    held, w5.at[slot, part], win_s.at[i], win_r.at[i], (t, to)
                )

    def relay(c):
        for k in range(TASKS):
            src = lax.rem(t - k + TASKS, TASKS)
            part = block(src, c)
            windows[0, c, k].wait_recv()
            i = 48 + 4 * c + k
            windows[3, c, k] = send(
                w5.at[2 - way, part], w5.at[2 - 2 * way, part],
                win_s.at[i], win_r.at[i], (t, mate),
            )

    for c in range(4):
        halo_copies[2 * c].wait_recv()
        halo_copies[2 * c + 1].wait_recv()
        lax.fori_loop(4 * c, 4 * c + 4, member, 0)
        exchange(c)
        if c == 3:
            rims = []
            for k in (1, 2, 3):
                rims.append(
                    send(
                        es.at[peer[k]], e5.at[2, t], rim_s.at[k - 1], rim_r.at[k - 1], (peer[k], s)
                    )
                )
            own_rim = pltpu.make_async_copy(es.at[t], e5.at[2, t], own.at[5])
            own_rim.start()
        if c:
            forward(c - 1)
    forward(3)
    for c in range(4):
        deepen(c)
    own_rim.wait()
    for copy in rims:
        copy.wait_recv()
    edges = [
        send(e5.at[2], e5.at[2 - d], edge_s.at[i], edge_r.at[i], (t, strip[d]))
        for i, d in enumerate((-2, -1, 1, 2))
    ]
    mine = pl.ds(pl.multiple_of(16 * t, 16), 16)

    def place(st):
        for src in range(TASKS):
            tile = e5[st, src]
            for m in range(16):
                rim[16 * src + m] = pltpu.roll(tile, (128 - 8 * m) % 128, 1) if m else tile
        rows = pl.ds(pl.multiple_of(8 * st, 8), 8)
        means, rim_means = [], []
        for r in range(8):
            whole = w5[st, :, r, :]
            mu = jnp.sum(whole, axis=0, keepdims=True) * (1.0 / 64)
            dev = whole - mu
            cols[4:260, st, r, :] = jnp.concatenate([dev, dev], axis=0).T
            means.append(mu)
            whole = rim[:, r, :]
            mu = jnp.sum(whole, axis=0, keepdims=True) * (1.0 / 64)
            dev = whole - mu
            turned = jnp.concatenate([dev, dev], axis=0).T
            cols[0:4, st, r, :] = turned[0:4]
            cols[260:264, st, r, :] = turned[4:8]
            rim_means.append(mu)
        mean[rows, 0:256] = jnp.concatenate(means, axis=0)
        mean[rows, 256:384] = jnp.concatenate(rim_means, axis=0)

    for copy in local:
        copy.wait()
    place(2)
    flat = jnp.concatenate([listed[0], listed[1]], axis=1)
    block_col = 4 * (iota((32, 128), 1) % 64) + 256 * t - 4
    code = ((flat // 8192 - (s - 2)) * 9 + flat % 8192 // 8 - block_col) * 8 + flat % 8
    pick = iota((64, 128), 0)
    into = iota((64, 128), 1)
    counts = live[...].astype(F32)
    alive = jnp.dot(
        counts, jnp.where(pick == into, 1.0, 0.0), preferred_element_type=F32
    )[0:1] + jnp.dot(counts, jnp.where(pick == into - 64, 1.0, 0.0), preferred_element_type=F32)[1:2]
    for slot in range(32):
        kept = jnp.where(alive > slot, code[slot : slot + 1, :], -100000)
        base[slot] = jnp.broadcast_to(kept, (8, 128)) - sub

    for copy in attr_copies:
        copy.wait()
    own_attr.wait()
    point_row = jnp.where(lane < 64, 1.5, 5.5)
    height = sub.astype(F32)
    taper[45] = jnp.zeros((8, 128), F32)

    def weigh(st, carry):
        for cr in range(9):
            q, shift = (cr - 4) % 4, (cr - 4) // 4
            row = spread(attr5[st, 0, 8 * q : 8 * q + 8, :], shift)
            value = spread(attr5[st, 1, 8 * q : 8 * q + 8, :], shift)
            var = spread(attr5[st, 2, 8 * q : 8 * q + 8, :], shift)
            tile = (st * 9 + cr) * 8
            count = jnp.zeros((8, 128), F32)
            for slot in range(32):
                count = count + jnp.where(base[slot] == tile, 1.0, 0.0)
            apart = row + (8.0 * (st - 2).astype(F32)) - point_row
            dist = apart * apart + (cr - 5.5) ** 2
            weight = count * jnp.exp(dist * (-1.0 / 1152.0)) / var
            pull = weight * value
            held = jnp.zeros((8, 128), F32)
            pulled = jnp.zeros((8, 128), F32)
            for k in range(8):
                hit = row[k : k + 1] == height
                held = held + jnp.where(hit, weight[k : k + 1], 0.0)
                pulled = pulled + jnp.where(hit, pull[k : k + 1], 0.0)
            taper[cr * 5 + st] = held
            force[cr * 5 + st] = pulled
        return carry

    lax.fori_loop(0, 5, weigh, 0)

    def field(lev, r):
        return w5[2, :, r, :] if lev == 0 else f1[:, lev - 1, r, :]

    def turn(lev):
        for r in range(8):
            whole = field(lev, r)
            dev = whole - jnp.sum(whole, axis=0, keepdims=True) * (1.0 / 64)
            turned[10:266, r // 2, 4 * (r % 2) + lev, :] = jnp.concatenate([dev, dev], axis=0).T

    total[...] = jnp.zeros_like(total)
    for ref in (mid, top, low):
        ref[...] = jnp.zeros_like(ref)
    turn(0)

    row = iota((8, 128), 0) // 4
    offset = jnp.where(lane < 64, 0.0, 4.0)
    first_strip = jnp.where(s == 0, 1.0, 0.0)
    last_strip = jnp.where(s == STRIPS - 1, 1.0, 0.0)

    def row_share(a, k):
        r = (2 * k + row).astype(F32)
        if a == -1:
            return hat(r + 4.0) * (1.0 - first_strip)
        if a == 0:
            return hat(r) + hat(r + 4.0) * first_strip
        if a == 1:
            return hat(r - 4.0) + hat(r - 8.0) * last_strip
        return hat(r - 8.0) * (1.0 - last_strip)

    left = iota((8, 8, 128), 2) < 64

    def parted(x, share):
        x = x * share[None]
        high = x.astype(BF16).astype(F32)
        return jnp.where(left, high, x - high)

    def part(n, carry):
        for k, a, ref in ((0, -1, top), (3, 1, low)):
            x = turned[pl.ds(8 * n + 10, 8), k]
            both = jnp.concatenate(
                [parted(x, row_share(a, k)), parted(x, row_share(a + 1, k))], axis=2
            )
            ref[pl.ds(pl.multiple_of(64 * n + 80, 16), 64)] = both.reshape(64, 256).astype(BF16)
        pieces = []
        for k in (1, 2):
            x = turned[pl.ds(8 * n + 10, 8), k]
            pieces.append(
                jnp.concatenate([parted(x, row_share(0, k)), parted(x, row_share(1, k))], axis=2)
            )
        both = jnp.stack(pieces, axis=1)
        mid[pl.ds(pl.multiple_of(128 * n + 160, 16), 128)] = both.reshape(128, 256).astype(BF16)
        return carry

    for copy in edges:
        copy.wait()
    for c in range(4):
        for k in range(TASKS):
            windows[2, c, k].wait_recv()
    place(2 + way)
    for c in range(4):
        relay(c)
    place(2 - way)
    for j, slot in ((1, 2 - 2 * way), (3, 2 + 2 * way)):
        for c in range(4):
            for k in range(TASKS):
                windows[j, c, k].wait_recv()
        place(slot)

    spot = iota((384, 128), 0)
    coarse = iota((384, 128), 1)
    lane_of = iota((40, 384), 1)
    known = jnp.where(lane_of < 264, mean[...], 0.0)
    for q in range(4):
        want = jnp.where(
            coarse == 0, 256 + q, jnp.where(coarse == 65, 260 + q, 4 * coarse - 4 + q)
        )
        picked[q] = jnp.dot(
            known,
            jnp.where((spot == want) & (coarse < 66), 1.0, 0.0),
            precision=lax.Precision.HIGHEST,
            preferred_element_type=F32,
        )
    def recentre(st, carry):
        for cr in range(9):
            q, shift = (cr - 4) % 4, (cr - 4) // 4
            centre = spread(picked[q, pl.ds(pl.multiple_of(8 * st, 8), 8), :], shift)
            force[cr * 5 + st] = force[cr * 5 + st] - taper[cr * 5 + st] * centre
        return carry

    lax.fori_loop(0, 5, recentre, 0)

    tall_lane = iota((368, 128), 1)
    eye = jnp.where(iota((64, 128), 0) == iota((64, 128), 1) % 64, 1.0, 0.0)

    def gram(b):
        index = jnp.where(lane < 64, b, 64 + b)
        near = cols[pl.ds(4 * b, 10)].reshape(400, 128)[:368]
        spread_taper = jnp.concatenate(
            [jnp.take_along_axis(taper[k], index, axis=1) for k in range(46)], axis=0
        )
        spread_force = jnp.concatenate(
            [jnp.take_along_axis(force[k], index, axis=1) for k in range(45)], axis=0
        )
        s_hi, s_lo = split(near * spread_taper)
        n_hi = near.astype(BF16).astype(F32)
        both = jnp.where(tall_lane < 64, n_hi, near - n_hi).astype(BF16)
        product = lax.dot_general(
            both,
            jnp.concatenate([s_hi, s_lo], axis=1),
            (((0,), (0,)), ((), ())),
            preferred_element_type=F32,
        )
        product = product[:64] + product[64:]
        return (
            product[:, :128] + product[:, 128:] + 63.0 * eye,
            jnp.sum(near[:360] * spread_force, axis=0, keepdims=True),
        )

    def keep(k, made):
        system[k] = made[0]
        drive[k] = jnp.broadcast_to(made[1], (8, 128))

    for k in range(GROUP):
        keep(k, gram(64 - GROUP + k))

    half = iota((64, 128), 1) < 64

    def rows_of(i):
        n = lax.rem(i + SOLVES - 1, SOLVES)
        part = pl.ds(1 + n * (GROUP // 2), GROUP // 2)
        return [
            sender(
                every.at[1 + a, part], every.at[3 - 3 * a, part],
                row_s.at[a, i], row_r.at[a, i], (t, (up, down)[a]),
            )
            for a in range(2)
        ]

    def sides_of():
        copies = []
        for i, (to, at, there) in enumerate(beyond):
            for a in range(2):
                copies.append(
                    sender(
                        every.at[1 + a, at + 1], every.at[1 + a, there],
                        side_s.at[2 * i + a], side_r.at[2 * i + a], (to, s),
                    )
                )
                copies.append(
                    sender(
                        every.at[1 + a, at + 1], every.at[3 - 3 * a, there],
                        corner_s.at[2 * i + a], corner_r.at[2 * i + a], (to, (up, down)[a]),
                    )
                )
        return copies

    def solve(i, carry):
        n = lax.rem(i + SOLVES - 1, SOLVES)
        nears, inverses, norms = [], [], []
        systems = [system[k] for k in range(GROUP)]
        drives = [drive[k][:1] for k in range(GROUP)]
        later = jnp.minimum(i, SOLVES - 2) * GROUP
        made = []

        def share(n):
            for k in range(n * GROUP // (2 * NS_ITERS), (n + 1) * GROUP // (2 * NS_ITERS)):
                made.append(gram(later + k))

        for x in systems:
            squares = jnp.sum(x * x, axis=0, keepdims=True)
            left = iota((1, 128), 1) < 64
            one = jnp.sum(jnp.where(left, squares, 0.0), axis=1, keepdims=True)
            two = jnp.sum(jnp.where(left, 0.0, squares), axis=1, keepdims=True)
            norm = jnp.sqrt(jnp.where(left, one, two))
            norms.append(norm)
            nears.append(x / norm)
            inverses.append(None)
        for turn in range(NS_ITERS):
            share(2 * turn)
            parts = [beside(x) for x in nears]
            weights = [doubled(x) for x in parts]
            if turn == 0:
                inverses = [1.5 * eye - 0.5 * x for x in nears]
                squared = [times(x, y) for x, y in zip(parts, weights)]
            elif turn < NS_ITERS - 1:
                squared = []
                for k in range(GROUP):
                    product = times(
                        jnp.concatenate([parts[k], beside(inverses[k])], axis=0), weights[k]
                    )
                    squared.append(product[:64])
                    inverses[k] = 1.5 * inverses[k] - 0.5 * product[64:]
            else:
                inverses = [
                    1.5 * x - 0.5 * times(beside(x), y) for x, y in zip(inverses, weights)
                ]
            share(2 * turn + 1)
            if turn < NS_ITERS - 1:
                nears = [
                    2.25 * x - 1.5 * y + 0.25 * times(beside(y), z)
                    for x, y, z in zip(nears, squared, weights)
                ]

        def standing(x):
            one = jnp.sum(jnp.where(half, x, 0.0), axis=1, keepdims=True)
            two = jnp.sum(jnp.where(half, 0.0, x), axis=1, keepdims=True)
            return jnp.where(half, one, two)

        finals = []
        for k in range(GROUP):
            z = inverses[k]
            once = jnp.sum(z * standing(eye * drives[k]), axis=0, keepdims=True)
            drift = standing(z * (once / norms[k]))
            finals.append(jnp.sqrt(63.0 / norms[k]) * z + drift)
        for k in range(0, GROUP, 2):
            g = n * (GROUP // 2) + k // 2
            every[1, g + 1] = jnp.where(half, finals[k], pltpu.roll(finals[k + 1], 64, 1))
            every[2, g + 1] = jnp.where(half, pltpu.roll(finals[k], 64, 1), finals[k + 1])
        for k in range(GROUP):
            keep(k, made[k])
        for copy in rows_of(i):
            copy.start()

        @pl.when(i == 1)
        def _():
            for copy in sides_of():
                copy.start()

        return carry

    def col_share(g):
        first = jnp.where((g == 0) & (t == 0), 1.0, 0.0)
        last = jnp.where((g == 31) & (t == TASKS - 1), 1.0, 0.0)
        alive = jnp.where(
            ((g == -1) & (t == 0)) | ((g == 32) & (t == TASKS - 1)), 0.0, 1.0
        )
        shares = []
        for c in range(12):
            x = (c - 2.0) - offset
            share = hat(x)
            if c in (2, 3):
                share = share + jnp.where(lane < 64, hat(x + 4.0), 0.0) * first
            if c in (8, 9):
                share = share + jnp.where(lane < 64, 0.0, hat(x - 4.0)) * last
            shares.append(share * alive)
        return shares

    def paired(x):
        hi, lo = split(x)
        zero = jnp.zeros((64, 128), BF16)
        return jnp.concatenate(
            [jnp.concatenate([hi, lo], axis=1), jnp.concatenate([hi, zero], axis=1)], axis=0
        )

    def blend(n, carry):
        g = n - 1
        shares = col_share(g)
        operands = [paired(every[a, n]) for a in range(4)]
        for a, ref, height, first in ((0, top, 8, 0), (1, mid, 16, 1), (2, low, 8, 3)):
            rows = ref[pl.ds(pl.multiple_of(height * (8 * g + 8), 16), 12 * height)]
            product = jnp.dot(
                rows,
                jnp.concatenate([operands[a], operands[a + 1]], axis=0),
                preferred_element_type=F32,
            )
            product = (product[:, :128] + product[:, 128:]).reshape(12, height // 8, 8, 128)
            for c in range(12):
                total[8 * g + 8 + c, first : first + height // 8] += product[c] * shares[c][None]
        return carry

    def finish(h):
        copies = []
        here = slice(128 * h, 128 * h + 128)
        ocean_cols = pl.ds(pl.multiple_of(256 * t + 128 * h, 128), 128)
        for r in range(8):
            ocean = wet[r : r + 1, ocean_cols].astype(F32)
            for lev in range(4):
                back = total[10 + 128 * h : 138 + 128 * h, r // 2, 4 * (r % 2) + lev, :].T
                whole = field(lev, r)[:, here]
                dev = whole - jnp.sum(whole, axis=0, keepdims=True) * (1.0 / 64)
                result[:, lev, r, here] = whole + ocean * (back[:64] + back[64:] - dev)
        copy = pltpu.make_async_copy(
            result.at[mine, :, :, here], out.at[:, :, :, ocean_cols], own.at[7 + h]
        )
        copy.start()
        copies.append(copy)
        for k in (1, 2, 3):
            theirs = pl.ds(pl.multiple_of(16 * peer[k], 16), 16)
            copies.append(
                send(
                    result.at[theirs, :, :, here], out.at[:, :, :, ocean_cols],
                    back_s.at[3 * h + k - 1], back_r.at[3 * h + k - 1], (peer[k], s),
                )
            )
        return copies

    lax.fori_loop(0, SOLVES - 1, solve, 0)

    for copy in own_deeps:
        copy.wait()
    for copy in deeps:
        copy.wait_recv()
    for lev in (1, 2, 3):
        turn(lev)
    lax.fori_loop(0, 32, part, 0)

    def arrived(i, carry):
        for copy in rows_of(i):
            copy.wait_recv()
        return carry

    sides = sides_of()
    lax.fori_loop(0, SOLVES - 2, arrived, 0)
    for copy in sides:
        copy.wait_recv()
    lax.fori_loop(0, 18, blend, 0)
    copies = finish(0)
    lax.fori_loop(SOLVES - 1, SOLVES, solve, 0)
    lax.fori_loop(SOLVES - 2, SOLVES, arrived, 0)
    lax.fori_loop(18, 34, blend, 0)
    copies += finish(1)

    def departed(i, carry):
        for copy in rows_of(i):
            copy.wait_send()
        return carry

    lax.fori_loop(0, SOLVES, departed, 0)
    for copy in sides + deeps + halo_copies + rims:
        copy.wait_send()
    for copy in swaps.values():
        copy.wait_send()
    for copy in windows.values():
        copy.wait_send()
    for copy in copies:
        copy.wait()


def assimilate(*arrays):
    dma = pltpu.SemaphoreType.DMA
    vmem = pl.BlockSpec(memory_space=pltpu.VMEM)
    return pl.pallas_call(
        kernel,
        out_shape=jax.ShapeDtypeStruct((16, 4, 8, 1024), F32),
        in_specs=[vmem] * 4 + [pl.BlockSpec(memory_space=pltpu.SMEM)] + [vmem] * 5,
        out_specs=pl.BlockSpec(memory_space=pl.ANY),
        scratch_shapes=[
            pltpu.VMEM((16, 4, 8, 1024), F32),
            pltpu.VMEM((8, 1024), jnp.int32),
            pltpu.VMEM((4, 2, 2, 8, 1024), F32),
            pltpu.VMEM((4, 8, 32, 128), F32),
            pltpu.VMEM((16, 8, 1024), F32),
            pltpu.VMEM((16, 3, 8, 1024), F32),
            pltpu.VMEM((4, 8, 128), F32),
            pltpu.VMEM((3, 32, 128), F32),
            pltpu.VMEM((5, 64, 8, 256), F32),
            pltpu.VMEM((5, 4, 8, 128), F32),
            pltpu.VMEM((5, 3, 32, 128), F32),
            pltpu.VMEM((64, 3, 8, 256), F32),
            pltpu.VMEM((4, 34, 64, 128), F32),
            pltpu.VMEM((264, 5, 8, 128), F32),
            pltpu.VMEM((64, 8, 128), F32),
            pltpu.VMEM((40, 384), F32),
            pltpu.VMEM((4, 40, 128), F32),
            pltpu.VMEM((32, 8, 128), jnp.int32),
            pltpu.VMEM((46, 8, 128), F32),
            pltpu.VMEM((45, 8, 128), F32),
            pltpu.VMEM((GROUP, 64, 128), F32),
            pltpu.VMEM((GROUP, 8, 128), F32),
            pltpu.VMEM((SPAN, 4, 8, 128), F32),
            pltpu.VMEM((SPAN * 16, 256), BF16),
            pltpu.VMEM((SPAN * 8, 256), BF16),
            pltpu.VMEM((SPAN * 8, 256), BF16),
            pltpu.VMEM((SPAN, 4, 8, 128), F32),
            pltpu.VMEM((64, 4, 8, 256), F32),
            dma((8,)), dma((8,)), dma((2,)), dma((2,)), dma((4,)), dma((4,)),
            dma((13,)), dma((12,)), dma((12,)), dma((3,)), dma((3,)),
            dma((64,)), dma((64,)), dma((4,)), dma((4,)),
            dma((12,)), dma((12,)), dma((2, SOLVES)), dma((2, SOLVES)),
            dma((4,)), dma((4,)), dma((4,)), dma((4,)), dma((6,)), dma((6,)),
        ],
        compiler_params=pltpu.CompilerParams(
            collective_id=0, has_side_effects=True, vmem_limit_bytes=LIMIT
        ),
    )(*arrays)


def body(
    trials_initial_dye,
    diffusivity,
    wet_mask,
    deeper_donor_tier,
    shallower_tier_fraction,
    obs_pos,
    obs_value,
    obs_var,
    observation_list,
    obs_count,
):
    return assimilate(
        trials_initial_dye,
        wet_mask,
        deeper_donor_tier,
        shallower_tier_fraction,
        diffusivity,
        obs_pos.reshape(64, 128),
        obs_value.reshape(64, 128),
        obs_var.reshape(64, 128),
        observation_list.transpose(0, 2, 1),
        obs_count,
    )


def solution(mesh):
    return jax.shard_map(
        body,
        mesh=mesh,
        in_specs=(
            P("task", None, "patch", None),
            P(),
            P("patch", None),
            P(None, "patch", None),
            P(None, "patch", None),
            P("patch"),
            P("patch"),
            P("patch"),
            P("patch", "task", None),
            P("patch", "task"),
        ),
        out_specs=P("task", None, "patch", None),
        check_vma=False,
    )
```
